128 devices in a mesh: seq: 32 (over x, y_hi, z), head: 4 (over y_lo, core).
Axes of the slice: x: 4, y: 4 (y_hi: 2, y_lo: 2; y = y_hi * 2 + y_lo), z: 4, core: 2. Of those that a mesh axis runs over, the one named last changes fastest.
Arguments:
- latents: bfloat16 [64, 12288], P(None, 'seq'), may hold values from -6 to 6
- span_ids: int32 [64], replicated, may hold values from 0 to 15, never falling along the last dimension, each value on 1 to 6 neighbouring positions
- patch_weight: bfloat16 [128, 3072], P(None, 'head'), may hold values from -0.5 to 0.5
- patch_bias: float32 [3072], P('head'), may hold values from -3 to 3
- norm_gain: float32 [3072], replicated, may hold values from 0.1 to 1.9
- query_weight: bfloat16 [3072, 3072], P(None, 'head'), may hold values from -1 to 1, as said below
- key_weight: bfloat16 [3072, 3072], P(None, 'head'), may hold values from -1 to 1
- value_weight: bfloat16 [3072, 3072], P(None, 'head'), may hold values from -0.109375 to 0.109375
- out_weight: bfloat16 [3072, 3072], P('head'), may hold values from -0.109375 to 0.109375
Outputs:
- layer_out: bfloat16 [12288, 3072], P('seq', 'head')
The draws below stay inside these ranges and needn't reach their ends.
Inputs may be any that keep to these rules, and one draw needn't show every extreme that they name: `query_weight`: entries of order 3072 ** -0.5.
All inputs are finite; a program needn't handle non-finite values.
Results may differ from the reference program's by a relative error of at most 0.012.
Values may be sent and summed in bfloat16 or wider, within the bound.
No kernel may reach another device: no remote copies, remote signals or barrier semaphores. Data moves between devices by JAX's collectives and lax.ppermute only.
A program may use at most 192 MiB of HBM per device.

```python
import math
import jax
import jax.numpy as jnp
import numpy as np
from jax import lax

D = 3072
HEADS = 24
HD = 128
LAT_W = 48
SPAN_MOST = 6
PATCH = 64
FT = 192
FRAMES = 64
TOKENS = 12288
SPANS = 16
N_HEAD = 4


def base_matrix(key):
    return jax.random.truncated_normal(jax.random.fold_in(key, 11), -4.0, 4.0, (D, D), jnp.float32) * D ** (-0.5)


def draw_query_weight(key, part):
    shared = base_matrix(key)
    return shared.astype(jnp.bfloat16)


def draw_key_weight(key, part):
    key = jax.random.fold_in(key, 2)
    own = jax.random.truncated_normal(jax.random.fold_in(key, 3), -4.0, 4.0, (D, D), jnp.float32) * D ** (-0.5)
    return (2.5 * own).astype(jnp.bfloat16)


def block_scale(stream_key, extent, cuts, least, high):
    def one(dim, parts):
        draws = jax.random.uniform(jax.random.fold_in(jax.random.fold_in(stream_key, 6), dim), (parts,), jnp.float32, least / len(cuts), high / len(cuts))
        return jnp.repeat(jnp.exp(draws), extent[dim] // parts).reshape((-1,) + (1,) * (len(extent) - dim - 1))

    gain = one(*cuts[0])
    for cut in cuts[1:]:
        gain = gain * one(*cut)
    return gain


def profile(number_of, total, most, lean):
    loads = [(1 << 20) // math.isqrt(grade ** lean) + 1 for grade in range(2, number_of + 1)]
    surplus, given = total - most - (number_of - 1), [1] * (number_of - 1)
    while surplus > 0:
        movable = [i for i in range(number_of - 1) if given[i] < most]
        whole, remaining = sum([loads[i] for i in movable]), surplus
        for i in movable:
            extra = min(most - given[i], max(1, remaining * loads[i] // whole), surplus)
            given[i] = given[i] + extra
            surplus = surplus - extra
    return np.array([most] + given)


def uneven(stream_key, number_of, total, limit, skew):
    if number_of == 2:
        one = jax.random.randint(stream_key, (), max(1, total - limit), min(limit, total - 1) + 1)
        return jnp.stack([one, total - one])
    tallies = jnp.asarray(profile(number_of, total, limit, skew), jnp.int32)
    couples = (number_of - 1) // 2
    source_of, taker = tallies[1:1 + 2 * couples:2], tallies[2:2 + 2 * couples:2]
    margin = jnp.minimum(source_of - 1, limit - taker)
    passed = jax.random.randint(jax.random.fold_in(stream_key, 1), (couples,), 0, 1 << 20) % (margin + 1)
    tallies = tallies.at[1:1 + 2 * couples:2].set(source_of - passed).at[2:2 + 2 * couples:2].set(taker + passed)
    return tallies[jax.random.permutation(jax.random.fold_in(stream_key, 2), number_of)]


def bell_draw(stream_key, dims, spread, bound, split=(), held_as=jnp.bfloat16):
    factor_of = block_scale(stream_key, dims, split, -0.22, 0.18) if split else 1.0
    array = jax.random.normal(stream_key, dims, jnp.float32) * spread * factor_of
    return jnp.minimum(jnp.maximum(array, -bound), bound).astype(held_as)


def setup_inputs(seed: int = 0) -> dict:
    splits = jax.random.split(jax.random.key(seed), 10)
    latents = bell_draw(splits[0], (PATCH, TOKENS), 1.0, 6.0, ((1, 32),))
    span_ids = jnp.searchsorted(jnp.cumsum(uneven(splits[1], SPANS, FRAMES, SPAN_MOST, 1)), jnp.arange(FRAMES), side="right").astype(jnp.int32)
    patch_weight = bell_draw(splits[2], (2 * PATCH, D), (2 * PATCH) ** -0.5, 0.5, ((1, 4),))
    patch_bias = bell_draw(splits[3], (D,), 0.5, 3.0, ((0, 4),), jnp.float32)
    norm_gain = jnp.clip(1.0 + 0.18 * jax.random.normal(splits[4], (D,), jnp.float32), 0.1, 1.9)
    query_weight = draw_query_weight(jax.random.fold_in(splits[9], 71), 0)
    key_weight = draw_key_weight(jax.random.fold_in(splits[9], 71), 0)
    value_weight = bell_draw(splits[7], (D, D), D ** -0.5, 0.109375, ((1, 4),))
    out_weight = bell_draw(splits[8], (D, D), D ** -0.5, 0.109375, ((0, 4),))
    return dict(latents=latents, span_ids=span_ids, patch_weight=patch_weight, patch_bias=patch_bias, norm_gain=norm_gain, query_weight=query_weight, key_weight=key_weight, value_weight=value_weight, out_weight=out_weight)


yarn_factor = 4.0
eps = 1e-06

def frame_table(frames):
    block = jnp.arange(frames).astype(jnp.int32)
    owner = block // 2
    return jnp.where(block % 2 == 0, owner, frames - 1 - owner).astype(jnp.int32)

def spectrum(count):
    steps = jnp.arange(count).astype(jnp.float32)
    return jnp.exp(-math.log(10000.0) * steps / count)

def rotary_angles(frame, row, col, pairs, frames):
    count_t = pairs // 4
    count_h = 3 * pairs // 8
    count_w = pairs - count_t - count_h
    base_t = spectrum(count_t)
    wave = 2.0 * math.pi / base_t
    ramp = jnp.clip((frames / 4.0 / wave - 1.0) / 31.0, 0.0, 1.0)
    scaled_t = base_t * (ramp + (1.0 - ramp) / yarn_factor)
    return jnp.concatenate([frame[:, None] * scaled_t[None, :], row[:, None] * spectrum(count_h)[None, :], col[:, None] * spectrum(count_w)[None, :]], axis=1)

def rotate(values, angles):
    pairs = angles.shape[1]
    cosine = jnp.cos(angles)[:, None, :]
    sine = jnp.sin(angles)[:, None, :]
    first = values[..., :pairs]
    second = values[..., pairs:]
    return jnp.concatenate([first * cosine - second * sine, first * sine + second * cosine], axis=-1)

def score_scale(head_size):
    return (0.1 * math.log(yarn_factor) + 1.0) ** 2 / math.sqrt(head_size)

def reference(latents, span_ids, patch_weight, patch_bias, norm_gain, query_weight, key_weight, value_weight, out_weight):
    frame_of = frame_table(FRAMES)
    place = jnp.zeros((FRAMES,), jnp.int32).at[frame_of].set(jnp.arange(FRAMES).astype(jnp.int32))
    stored = latents.reshape(PATCH, FRAMES, FT)
    natural = jnp.take(stored, place, axis=1)
    before = jnp.concatenate([jnp.zeros((PATCH, 1, FT), latents.dtype), natural[:, :-1]], axis=1)
    patches = jnp.concatenate([before, natural], axis=0).reshape(2 * PATCH, TOKENS)
    conv = lax.dot_general(patches, patch_weight, (((0,), (0,)), ((), ())), preferred_element_type=jnp.float32)
    tokens = (conv + patch_bias[None, :]).astype(jnp.bfloat16)
    wide = tokens.astype(jnp.float32)
    mean_sq = lax.optimization_barrier(jnp.mean(wide * wide, axis=1, keepdims=True))
    normed = (wide * lax.rsqrt(mean_sq + eps) * norm_gain[None, :]).astype(jnp.bfloat16)
    position = jnp.arange(TOKENS).astype(jnp.int32)
    frame = position // FT
    inner = position % FT
    half_w = LAT_W // 2
    angles = rotary_angles(frame.astype(jnp.float32), (inner // half_w).astype(jnp.float32), (inner % half_w).astype(jnp.float32), HD // 2, FRAMES)
    query = rotate(jnp.dot(normed, query_weight, preferred_element_type=jnp.float32).reshape(TOKENS, HEADS, HD), angles).astype(jnp.bfloat16)
    keys = rotate(jnp.dot(normed, key_weight, preferred_element_type=jnp.float32).reshape(TOKENS, HEADS, HD), angles).astype(jnp.bfloat16)
    values = jnp.dot(normed, value_weight, preferred_element_type=jnp.float32).astype(jnp.bfloat16).reshape(TOKENS, HEADS, HD)
    token_span = jnp.repeat(span_ids, FT)
    keys_wide = keys.astype(jnp.float32)
    values_wide = values.astype(jnp.float32)
    scale = score_scale(HD)

    def one_frame(inputs):
        query_block, query_span = inputs
        scores = jnp.einsum('qhd,khd->hqk', query_block.astype(jnp.float32), keys_wide) * scale
        allowed = (token_span <= query_span)[None, None, :]
        scores = jnp.where(allowed, scores, -1e+30)
        top = lax.optimization_barrier(jnp.max(scores, axis=2, keepdims=True))
        weights = jnp.where(allowed, jnp.exp(scores - top), 0.0)
        total = lax.optimization_barrier(jnp.sum(weights, axis=2))
        rounded = lax.optimization_barrier(weights.astype(jnp.bfloat16)).astype(jnp.float32)
        mixed = jnp.einsum('hqk,khd->qhd', rounded, values_wide)
        return (mixed / jnp.transpose(total)[:, :, None]).astype(jnp.bfloat16)
    attended = lax.map(one_frame, (query.reshape(FRAMES, FT, HEADS, HD), span_ids))
    heads_out = attended.reshape(TOKENS, D)
    group = D // N_HEAD
    summed = tokens.astype(jnp.float32)
    for index in range(N_HEAD):
        piece = heads_out[:, index * group:(index + 1) * group]
        rows = out_weight[index * group:(index + 1) * group, :]
        partial_sum = jnp.dot(piece, rows, preferred_element_type=jnp.float32)
        summed = summed + lax.optimization_barrier(partial_sum.astype(jnp.bfloat16)).astype(jnp.float32)
    result = summed.astype(jnp.bfloat16).reshape(FRAMES, FT, D)
    return jnp.take(result, frame_of, axis=0).reshape(TOKENS, D)
```

```python
import functools
import math

import jax
import jax.numpy as jnp
import numpy as np
from jax import lax
from jax.experimental import pallas as pl
from jax.experimental.pallas import tpu as pltpu
from jax.sharding import PartitionSpec as P

HD = 128
HEADS = 6
FT = 192
FRAMES = 64
BF = 4
BK = BF * FT
NB = FRAMES // BF
ROWS = 144
WIDTH = 24
EPS = 1e-06
YARN = 4.0
SCALE = (0.1 * math.log(YARN) + 1.0) ** 2 / math.sqrt(HD) * math.log2(math.e)
FAR = -1e30
LOW, HIGH = 2.0**-60, 2.0**100

F32 = jnp.float32
BF16 = jnp.bfloat16


def spectrum(count):
    return np.exp(-math.log(10000.0) * np.arange(count) / count)


def frequencies():
    pairs = HD // 2
    count_t, count_h = pairs // 4, 3 * pairs // 8
    base_t = spectrum(count_t)
    ramp = np.clip((FRAMES / 4.0 / (2.0 * math.pi / base_t) - 1.0) / 31.0, 0.0, 1.0)
    return base_t * (ramp + (1.0 - ramp) / YARN), spectrum(count_h), spectrum(pairs - count_t - count_h)


def spatial_angles():
    _, w_h, w_w = frequencies()
    inner = np.arange(FT)
    return np.concatenate(
        [np.outer(inner // WIDTH, w_h), np.outer(inner % WIDTH, w_w)], axis=1
    )


def dot(a, b):
    return jnp.dot(a, b, preferred_element_type=F32)


def kernel(
    meta,
    x_ref,
    ghi_ref,
    glo_ref,
    mk_ref,
    mq_ref,
    mv_ref,
    cs_ref,
    ss_ref,
    ct_ref,
    st_ref,
    cq_ref,
    sq_ref,
    wo_ref,
    out_ref,
    u_ref,
    q_ref,
    own_ref,
    ho_ref,
    m_ref,
):
    end_early, end_late = meta[0], meta[1]
    blocks_early = (end_early + BF - 1) // BF
    blocks_late = (end_late + BF - 1) // BF

    def prepare(b):
        x = x_ref[b]
        row = lax.broadcasted_iota(jnp.int32, (ROWS - 128, BK), 0)
        full = jnp.concatenate([x, (row < 3).astype(F32).astype(BF16)], axis=0)
        y = dot(ghi_ref[...], full) + dot(glo_ref[...], full)
        mean_sq = jnp.sum(full.astype(F32) * y, axis=0, keepdims=True)
        r = lax.rsqrt(mean_sq + EPS)
        tail = jnp.where(row == 0, r, jnp.where(row == 1, 1.0, 0.0))
        at = jnp.concatenate([x.astype(F32) * r, tail], axis=0)
        return at.astype(BF16), at.T.astype(BF16)

    def keys_of(b, at, h):
        pre = dot(mk_ref[pl.ds(h * HD, HD), :], at)
        cos = jnp.concatenate([ct_ref[b], cs_ref[...]], axis=0)
        sin = jnp.concatenate([st_ref[b], ss_ref[...]], axis=0)
        first, second = pre[:64], pre[64:]
        rotated = jnp.concatenate(
            [first * cos - second * sin, first * sin + second * cos], axis=0
        ).astype(BF16)
        row = lax.broadcasted_iota(jnp.int32, (ROWS - 128, BK), 0)
        frame = b * BF + lax.broadcasted_iota(jnp.int32, (ROWS - 128, BK), 1) // FT
        end = jnp.where(row == 0, end_early, end_late)
        mask = jnp.where((row < 2) & (frame >= end), FAR, 0.0).astype(BF16)
        return jnp.concatenate([rotated, mask], axis=0)

    for i in range(2):
        frame = meta[2 + i]
        _, av = prepare(frame // BF)
        own_ref[...] = av
        own = own_ref[pl.ds(pl.multiple_of((frame % BF) * FT, FT), FT), :]
        lane = lax.broadcasted_iota(jnp.int32, (FT, ROWS - 128), 1)
        select = (lane == i).astype(F32).astype(BF16)
        for h in range(HEADS):
            pre = dot(own, mq_ref[:, pl.ds(h * HD, HD)])
            rotated = pre * cq_ref[i] + pltpu.roll(pre, 64, 1) * sq_ref[i]
            q_ref[h, pl.ds(i * FT, FT), :] = jnp.concatenate(
                [rotated.astype(BF16), select], axis=1
            )

    u_ref[...] = jnp.zeros_like(u_ref)

    def visit(rows, b, carry):
        at, av = prepare(b)
        for h in range(HEADS):
            s = dot(q_ref[h, rows, :], keys_of(b, at, h))
            w = jnp.exp2(s).astype(BF16)
            u_ref[h, rows, :] += dot(w, av)
        return carry

    lax.fori_loop(0, blocks_early, functools.partial(visit, pl.ds(0, 2 * FT)), 0)
    lax.fori_loop(blocks_early, blocks_late, functools.partial(visit, pl.ds(FT, FT)), 0)

    total = u_ref[:, :, 129:130]
    good = jnp.where((total >= LOW) & (total <= HIGH), 1.0, 0.0)
    bad = jnp.min(good) < 0.5

    @pl.when(bad)
    def _():
        u_ref[...] = jnp.zeros_like(u_ref)
        m_ref[...] = jnp.full_like(m_ref, FAR)

        def visit_again(b, carry):
            at, av = prepare(b)
            for h in range(HEADS):
                s = dot(q_ref[h], keys_of(b, at, h))
                old = m_ref[h]
                new = jnp.maximum(old, jnp.max(s, axis=1, keepdims=True))
                w = jnp.exp2(s - new).astype(BF16)
                u_ref[h] = u_ref[h] * jnp.exp2(old - new) + dot(w, av)
                m_ref[h] = new
            return carry

        lax.fori_loop(0, blocks_late, visit_again, 0)

    for h in range(HEADS):
        u = u_ref[h]
        mixed = (u / u[:, 129:130]).astype(BF16)
        ho_ref[:, pl.ds(h * HD, HD)] = dot(mixed, mv_ref[:, pl.ds(h * HD, HD)]).astype(BF16)
    for n in range(4):
        out_ref[n] = dot(ho_ref[...], wo_ref[:, pl.ds(n * 768, 768)]).astype(BF16)


def attention(meta, *arrays):
    vmem = pl.BlockSpec(memory_space=pltpu.VMEM)
    return pl.pallas_call(
        kernel,
        in_specs=[pl.BlockSpec(memory_space=pltpu.SMEM)] + [vmem] * len(arrays),
        out_specs=vmem,
        out_shape=jax.ShapeDtypeStruct((4, 2 * FT, 768), BF16),
        scratch_shapes=[
            pltpu.VMEM((HEADS, 2 * FT, ROWS), F32),
            pltpu.VMEM((HEADS, 2 * FT, ROWS), BF16),
            pltpu.VMEM((BK, ROWS), BF16),
            pltpu.VMEM((2 * FT, HEADS * HD), BF16),
            pltpu.VMEM((HEADS, 2 * FT, 1), F32),
        ],
        compiler_params=pltpu.CompilerParams(vmem_limit_bytes=56 * 2**20),
    )(meta, *arrays)


def permute(x, axis, to):
    return lax.ppermute(x, axis, [(i, to(i)) for i in range(lax.axis_size(axis))])


def in_turn(parts, at, axis):
    n = len(parts)
    turned = [parts[-r % n] for r in range(n)]
    doubled = jnp.stack(turned + turned[:-1], axis=axis)
    return lax.dynamic_slice_in_dim(doubled, (n - at) % n, n, axis)


def all_latents(latents):
    seq, core = lax.axis_index("seq"), lax.axis_index("head") % 2
    x, y, z = seq // 8, (seq // 4) % 2, seq % 4

    def place(i):
        return i // 8, (i // 4) % 2, i % 4

    def at(x, y, z):
        return (x * 2 + y) * 4 + z

    def to_y(i):
        x, y, z = place(i)
        return at(x, 1 - y, z)

    def to_z(k, i):
        x, y, z = place(i)
        return at(x, y, (z + k) % 4)

    def to_x(k, i):
        x, y, z = place(i)
        return at((x + k) % 4, y, z)

    block = lax.dynamic_slice_in_dim(latents, core * 32, 32, 0)
    block = in_turn([block, permute(block, "seq", to_y)], y, 0)
    parts = [block] + [permute(block, "seq", functools.partial(to_z, k)) for k in (1, 2, 3)]
    block = in_turn(parts, z, 1)
    parts = [block] + [permute(block, "seq", functools.partial(to_x, k)) for k in (1, 2, 3)]
    block = in_turn(parts, x, 0)
    other = permute(block, "head", lambda i: i ^ 1)
    block = in_turn([block, other], core, 3)
    block = block.reshape(32, 64, 2 * FT)
    return jnp.concatenate([block[:, :, :FT], block[::-1, :, FT:]], axis=0)


def all_channels(weight):
    me = lax.axis_index("head")
    parts = [weight] + [permute(weight, "head", lambda i, k=k: (i + k) % 4) for k in (1, 2, 3)]
    block = in_turn(parts, me, 1)
    return block.reshape(weight.shape[0], 4 * weight.shape[1])


def sum_scatter(parts):
    me = lax.axis_index("head")
    core, chip = me % 2, me // 2
    pairs = parts.reshape(2, 2, *parts.shape[1:])
    mine = lax.dynamic_index_in_dim(pairs, core, 1, False)
    other = permute(lax.dynamic_index_in_dim(pairs, 1 - core, 1, False), "head", lambda i: i ^ 1)
    both = (mine.astype(F32) + other.astype(F32)).astype(BF16)
    mine = lax.dynamic_index_in_dim(both, chip, 0, False)
    other = permute(lax.dynamic_index_in_dim(both, 1 - chip, 0, False), "head", lambda i: i ^ 2)
    return mine.astype(F32) + other.astype(F32)


def local(
    latents,
    span_ids,
    patch_weight,
    patch_bias,
    norm_gain,
    query_weight,
    key_weight,
    value_weight,
    out_weight,
):
    seq = lax.axis_index("seq")
    frames = jnp.stack([seq, FRAMES - 1 - seq]).astype(jnp.int32)
    own_span = jnp.sum(jnp.where(frames[:, None] == jnp.arange(FRAMES)[None], span_ids[None], 0), axis=1)
    ends = jnp.sum((span_ids[None, :] <= own_span[:, None]).astype(jnp.int32), axis=1)
    meta = jnp.concatenate([ends, frames])

    natural = all_latents(latents)
    before = jnp.concatenate([jnp.zeros((1, 64, FT), BF16), natural[:-1]], axis=0)
    patches = jnp.concatenate([before, natural], axis=1)
    x = patches.reshape(NB, BF, 128, FT).transpose(0, 2, 1, 3).reshape(NB, 128, BK)

    b0 = patch_bias.astype(BF16)
    b1 = (patch_bias - b0.astype(F32)).astype(BF16)
    b2 = (patch_bias - b0.astype(F32) - b1.astype(F32)).astype(BF16)
    rest = jnp.zeros((ROWS - 131, patch_bias.shape[0]), BF16)
    wide = all_channels(jnp.concatenate([patch_weight, b0[None], b1[None], b2[None], rest], axis=0))
    gram = lax.dot_general(wide, wide, (((1,), (1,)), ((), ())), preferred_element_type=F32)
    gram = gram * (1.0 / wide.shape[1])
    ghi = gram.astype(BF16)
    glo = (gram - ghi.astype(F32)).astype(BF16)
    bias = jnp.sum(wide[128:131].astype(F32), axis=0, keepdims=True)
    row = jnp.arange(ROWS)[:, None]
    gained = jnp.where(row < 128, wide.astype(F32), jnp.where(row == 128, bias, 0.0))
    gained = (gained * norm_gain[None]).astype(BF16)
    mq = dot(gained, query_weight).astype(BF16)
    mv = dot(gained, value_weight).astype(BF16)
    mk = lax.dot_general(
        key_weight, gained, (((0,), (1,)), ((), ())), preferred_element_type=F32
    ).astype(BF16)

    w_t, _, _ = frequencies()
    spatial = spatial_angles()
    cs = jnp.asarray(np.tile(np.cos(spatial).T, (1, BF)), F32)
    ss = jnp.asarray(np.tile(np.sin(spatial).T, (1, BF)), F32)
    temporal = np.outer(np.arange(FRAMES), w_t)
    by_block = np.repeat(temporal.reshape(NB, BF, 16).transpose(0, 2, 1), FT, axis=2)
    ct = jnp.asarray(np.cos(by_block), F32)
    st = jnp.asarray(np.sin(by_block), F32)
    angle = frames.astype(F32)[:, None] * jnp.asarray(w_t, F32)[None]

    def of_queries(turn, space):
        own = jnp.broadcast_to(turn[:, None, :], (2, FT, 16))
        return jnp.concatenate([own, jnp.broadcast_to(jnp.asarray(space, F32)[None], (2, FT, 48))], axis=2) * SCALE

    cq = of_queries(jnp.cos(angle), np.cos(spatial))
    sq = of_queries(jnp.sin(angle), np.sin(spatial))
    cq = jnp.concatenate([cq, cq], axis=2)
    sq = jnp.concatenate([-sq, sq], axis=2)

    parts = attention(meta, x, ghi, glo, mk, mq, mv, cs, ss, ct, st, cq, sq, out_weight)
    summed = sum_scatter(parts)

    own = jnp.concatenate(
        [lax.dynamic_index_in_dim(patches, frames[i], 0, False) for i in range(2)], axis=1
    )
    conv = lax.dot_general(own, patch_weight, (((0,), (0,)), ((), ())), preferred_element_type=F32)
    tokens = (conv + patch_bias[None, :]).astype(BF16)
    return (summed + tokens.astype(F32)).astype(BF16)


def solution(mesh):
    return jax.shard_map(
        local,
        mesh=mesh,
        in_specs=(
            P(None, "seq"),
            P(),
            P(None, "head"),
            P("head"),
            P(),
            P(None, "head"),
            P(None, "head"),
            P(None, "head"),
            P("head", None),
        ),
        out_specs=P("seq", "head"),
        check_vma=False,
    )
```

```python
import functools
import math

import jax
import jax.numpy as jnp
import numpy as np
from jax import lax
from jax.experimental import pallas as pl
from jax.experimental.pallas import tpu as pltpu
from jax.sharding import PartitionSpec as P

HD = 128
HEADS = 6
FT = 192
FRAMES = 64
BF = 4
BK = BF * FT
NB = FRAMES // BF
ROWS = 144
WIDTH = 24
EPS = 1e-06
YARN = 4.0
SCALE = (0.1 * math.log(YARN) + 1.0) ** 2 / math.sqrt(HD) * math.log2(math.e)
FAR = -1e30
LOW, HIGH = 2.0**-60, 2.0**100

F32 = jnp.float32
BF16 = jnp.bfloat16


def spectrum(count):
    return np.exp(-math.log(10000.0) * np.arange(count) / count)


def frequencies():
    pairs = HD // 2
    count_t, count_h = pairs // 4, 3 * pairs // 8
    base_t = spectrum(count_t)
    ramp = np.clip((FRAMES / 4.0 / (2.0 * math.pi / base_t) - 1.0) / 31.0, 0.0, 1.0)
    return base_t * (ramp + (1.0 - ramp) / YARN), spectrum(count_h), spectrum(pairs - count_t - count_h)


def spatial_angles():
    _, w_h, w_w = frequencies()
    inner = np.arange(FT)
    return np.concatenate(
        [np.outer(inner // WIDTH, w_h), np.outer(inner % WIDTH, w_w)], axis=1
    )


def dot(a, b):
    return jnp.dot(a, b, preferred_element_type=F32)


def kernel(
    meta,
    *refs,
):
    pieces, refs = refs[:8], refs[8:]
    (mg_ref, mq_ref, mv_ref, pw_ref, cs_ref, ss_ref, ct_ref, st_ref, cq_ref, sq_ref, wo_ref) = refs[:11]
    (outs, tokens_ref), refs = (refs[11:15], refs[15]), refs[16:]
    raw_ref, wide_ref, own_ref, q_ref, w_ref, u_ref, ho_ref, m_ref, sems, wo_sem = refs
    end_early, end_late = meta[0], meta[1]
    blocks_early = (end_early + BF - 1) // BF
    blocks_late = (end_late + BF - 1) // BF
    x_at, y_at, core, chip = meta[4], meta[5], meta[6], meta[7]

    out_copy = pltpu.make_async_copy(wo_ref, wide_ref, wo_sem)
    out_copy.start()
    copies = []
    for k in range(4):
        for c in range(2):
            rows = pl.ds(pl.multiple_of((core ^ c) * 32, 32), 32)
            for i in range(2):
                group = ((x_at + 4 - k) % 4) * 2 + (y_at ^ i)
                for late in range(2):
                    block = NB - 1 - group if late else group
                    copies.append(
                        pltpu.make_async_copy(
                            pieces[2 * k + c].at[i, late],
                            raw_ref.at[block, rows],
                            sems.at[len(copies)],
                        )
                    )
    for copy in copies:
        copy.start()
    for copy in copies:
        copy.wait()

    row = lax.broadcasted_iota(jnp.int32, (ROWS - 128, BK), 0)
    lane_frame = lax.broadcasted_iota(jnp.int32, (ROWS - 128, BK), 1) // FT
    ones = (row < 3).astype(F32).astype(BF16)

    def features(b):
        now = raw_ref[b]
        last = raw_ref[jnp.maximum(b - 1, 0)][:, BK - FT :]
        last = jnp.where(b > 0, last, jnp.zeros_like(last))
        before = jnp.concatenate([last, now[:, : BK - FT]], axis=1)
        return jnp.concatenate([before, now, ones], axis=0)

    def norm(x, gram):
        y = gram[:ROWS] + gram[ROWS:]
        return lax.rsqrt(jnp.sum(x.astype(F32) * y, axis=0, keepdims=True) + EPS)

    def scaled(x, r):
        tail = jnp.where(row == 0, r, jnp.where(row == 1, 1.0, 0.0))
        return jnp.concatenate([x[:128].astype(F32) * r, tail], axis=0).astype(BF16).T

    def prepare(b):
        x = features(b)
        big = dot(mg_ref[...], x)
        r = norm(x, big[HEADS * HD :])
        cos = jnp.concatenate([ct_ref[b], cs_ref[...]], axis=0) * r
        sin = jnp.concatenate([st_ref[b], ss_ref[...]], axis=0) * r
        end = jnp.where(row == 0, end_early, end_late)
        mask = jnp.where((row < 2) & (b * BF + lane_frame >= end), FAR, 0.0).astype(BF16)

        def keys(h):
            first, second = big[h * HD : h * HD + 64], big[h * HD + 64 : h * HD + HD]
            return jnp.concatenate(
                [
                    (first * cos - second * sin).astype(BF16),
                    (first * sin + second * cos).astype(BF16),
                    mask,
                ],
                axis=0,
            )

        return keys, scaled(x, r)

    for i in range(2):
        frame = meta[2 + i]
        rows = pl.ds(pl.multiple_of((frame % BF) * FT, FT), FT)
        x = features(frame // BF)
        own_ref[...] = x.T
        tokens_ref[pl.ds(i * FT, FT), :] = dot(own_ref[rows, :], pw_ref[...]).astype(BF16)
        own_ref[...] = scaled(x, norm(x, dot(mg_ref[HEADS * HD :], x)))
        own = own_ref[rows, :]
        lane = lax.broadcasted_iota(jnp.int32, (FT, ROWS - 128), 1)
        select = (lane == i).astype(F32).astype(BF16)
        for h in range(HEADS):
            pre = dot(own, mq_ref[:, pl.ds(h * HD, HD)])
            rotated = pre * cq_ref[i] + pltpu.roll(pre, 64, 1) * sq_ref[i]
            q_ref[i, h] = jnp.concatenate([rotated.astype(BF16), select], axis=1)

    u_ref[...] = jnp.zeros_like(u_ref)

    def visit(frames, b, carry):
        keys, av = prepare(b)
        for h in range(HEADS):
            q = jnp.concatenate([q_ref[i, h] for i in frames], axis=0)
            w = jnp.exp2(dot(q, keys(h))).astype(BF16)
            for n, i in enumerate(frames):
                w_ref[i, pl.ds(h * FT, FT)] = w[n * FT : (n + 1) * FT]
        for i in frames:
            u_ref[i] += dot(w_ref[i], av)
        return carry

    lax.fori_loop(0, blocks_early, functools.partial(visit, (0, 1)), 0)
    lax.fori_loop(blocks_early, blocks_late, functools.partial(visit, (1,)), 0)

    total = u_ref[:, :, 129:130]
    good = jnp.where((total >= LOW) & (total <= HIGH), 1.0, 0.0)
    bad = jnp.min(good) < 0.5

    @pl.when(bad)
    def _():
        u_ref[...] = jnp.zeros_like(u_ref)
        m_ref[...] = jnp.full_like(m_ref, FAR)

        def visit_again(b, carry):
            keys, av = prepare(b)
            for h in range(HEADS):
                k = keys(h)
                rows = pl.ds(h * FT, FT)
                for i in range(2):
                    s = dot(q_ref[i, h], k)
                    old = m_ref[i, rows]
                    new = jnp.maximum(old, jnp.max(s, axis=1, keepdims=True))
                    w = jnp.exp2(s - new).astype(BF16)
                    u_ref[i, rows] = u_ref[i, rows] * jnp.exp2(old - new) + dot(w, av)
                    m_ref[i, rows] = new
            return carry

        lax.fori_loop(0, blocks_late, visit_again, 0)

    for i in range(2):
        for h in range(HEADS):
            u = u_ref[i, pl.ds(h * FT, FT)]
            mixed = (u / u[:, 129:130]).astype(BF16)
            ho_ref[pl.ds(i * FT, FT), pl.ds(h * HD, HD)] = dot(
                mixed, mv_ref[:, pl.ds(h * HD, HD)]
            ).astype(BF16)
    out_copy.wait()
    for n, ref in enumerate(outs):
        group = (chip ^ (n // 2)) * 2 + (core ^ (n % 2))
        columns = pl.ds(pl.multiple_of(group * 768, 768), 768)
        ref[...] = dot(ho_ref[...], wide_ref[:, columns]).astype(BF16)


def attention(meta, *arrays):
    vmem = pl.BlockSpec(memory_space=pltpu.VMEM)
    hbm = pl.BlockSpec(memory_space=pl.ANY)
    shape = jax.ShapeDtypeStruct((2 * FT, 768), BF16)
    return pl.pallas_call(
        kernel,
        in_specs=[pl.BlockSpec(memory_space=pltpu.SMEM)] + [hbm] * 8 + [vmem] * 10 + [hbm],
        out_specs=(vmem,) * 5,
        out_shape=(shape,) * 5,
        scratch_shapes=[
            pltpu.VMEM((NB, 64, BK), BF16),
            pltpu.VMEM((768, 3072), BF16),
            pltpu.VMEM((BK, ROWS), BF16),
            pltpu.VMEM((2, HEADS, FT, ROWS), BF16),
            pltpu.VMEM((2, HEADS * FT, BK), BF16),
            pltpu.VMEM((2, HEADS * FT, ROWS), F32),
            pltpu.VMEM((2 * FT, HEADS * HD), BF16),
            pltpu.VMEM((2, HEADS * FT, 1), F32),
            pltpu.SemaphoreType.DMA((32,)),
            pltpu.SemaphoreType.DMA,
        ],
        compiler_params=pltpu.CompilerParams(vmem_limit_bytes=56 * 2**20),
    )(meta, *arrays)


def permute(x, axis, to):
    return lax.ppermute(x, axis, [(i, to(i)) for i in range(lax.axis_size(axis))])


def weights_kernel(me, p0, p1, p2, p3, gain, wq, wk, wv, mg_ref, mq_ref, mv_ref, aq, ak, av, ag):
    k = pl.program_id(0)

    @pl.when(k == 0)
    def _():
        for ref in (aq, ak, av, ag):
            ref[...] = jnp.zeros_like(ref)

    part = jnp.where(k < 2, jnp.where(k == 0, p0[...], p1[...]), jnp.where(k == 2, p2[...], p3[...]))
    wide = part.astype(F32)
    bias = wide[128:129] + wide[129:130] + wide[130:131]
    row = lax.broadcasted_iota(jnp.int32, (ROWS - 128, part.shape[1]), 0)
    gained = jnp.concatenate([wide[:128], jnp.where(row == 0, bias, 0.0)], axis=0) * gain[0]
    gained = gained.astype(BF16)
    aq[...] += dot(gained, wq[...])
    ak[...] += dot(gained, wk[...])
    av[...] += dot(gained, wv[...])
    ag[...] += lax.dot_general(part, part, (((1,), (1,)), ((), ())), preferred_element_type=F32)

    @pl.when(k == 3)
    def _():
        mq_ref[...] = aq[...].astype(BF16)
        mv_ref[...] = av[...].astype(BF16)
        mg_ref[: HEADS * HD, :] = ak[...].T.astype(BF16)
        gram = ag[...] * (1.0 / (4 * part.shape[1]))
        high = gram.astype(BF16)
        mg_ref[HEADS * HD : HEADS * HD + ROWS, :] = high
        mg_ref[HEADS * HD + ROWS :, :] = (gram - high.astype(F32)).astype(BF16)


def through(parts, gain, wq, wk, wv):
    columns = HEADS * HD
    whole = lambda *shape: pl.BlockSpec(shape, lambda k, me: (0,) * len(shape))
    source = lambda k, me: (me[0] + 4 - k) % 4
    weight = pl.BlockSpec((columns, columns), lambda k, me: (source(k, me), 0))
    return pl.pallas_call(
        weights_kernel,
        grid_spec=pltpu.PrefetchScalarGridSpec(
            num_scalar_prefetch=1,
            grid=(4,),
            in_specs=[whole(ROWS, columns)] * 4
            + [pl.BlockSpec((1, 1, columns), lambda k, me: (source(k, me), 0, 0))]
            + [weight] * 3,
            out_specs=[
                whole(columns + 2 * ROWS, ROWS),
                whole(ROWS, columns),
                whole(ROWS, columns),
            ],
            scratch_shapes=[pltpu.VMEM((ROWS, columns), F32)] * 3 + [pltpu.VMEM((ROWS, ROWS), F32)],
        ),
        out_shape=[
            jax.ShapeDtypeStruct((columns + 2 * ROWS, ROWS), BF16),
            jax.ShapeDtypeStruct((ROWS, columns), BF16),
            jax.ShapeDtypeStruct((ROWS, columns), BF16),
        ],
        compiler_params=pltpu.CompilerParams(vmem_limit_bytes=24 * 2**20),
        cost_estimate=pl.CostEstimate(
            flops=2 * ROWS * 3072 * 2400, bytes_accessed=3 * 3072 * 768 * 2, transcendentals=0
        ),
    )(lax.axis_index("head").astype(jnp.int32).reshape(1), *parts, gain.reshape(4, 1, columns), wq, wk, wv)


def join_kernel(z, p0, p1, p2, p3, out):
    for place in range(4):
        k = (z[0] + 4 - place) % 4
        part = jnp.where(k < 2, jnp.where(k == 0, p0[...], p1[...]), jnp.where(k == 2, p2[...], p3[...]))
        out[0, :, place * FT : (place + 1) * FT] = part[:, :FT]
        out[1, :, (3 - place) * FT : (4 - place) * FT] = part[:, FT:]


def join(z, parts):
    vmem = pl.BlockSpec(memory_space=pltpu.VMEM)
    return pl.pallas_call(
        join_kernel,
        in_specs=[pl.BlockSpec(memory_space=pltpu.SMEM)] + [vmem] * 4,
        out_specs=vmem,
        out_shape=jax.ShapeDtypeStruct((2, 32, BK), BF16),
        cost_estimate=pl.CostEstimate(flops=0, bytes_accessed=200000, transcendentals=0),
    )(z.astype(jnp.int32).reshape(1), *parts)


def all_latents(latents):
    seq, core = lax.axis_index("seq"), lax.axis_index("head") % 2

    def place(i):
        return i // 8, (i // 4) % 2, i % 4

    def at(x, y, z):
        return (x * 2 + y) * 4 + z

    def to_y(i):
        x, y, z = place(i)
        return at(x, 1 - y, z)

    def to_z(k, i):
        x, y, z = place(i)
        return at(x, y, (z + k) % 4)

    def to_x(k, i):
        x, y, z = place(i)
        return at((x + k) % 4, y, z)

    half = lax.dynamic_slice_in_dim(latents, core * 32, 32, 0)
    parts = [half] + [permute(half, "seq", functools.partial(to_z, k)) for k in (1, 2, 3)]
    block = join(seq % 4, parts)
    pair = jnp.stack([block, permute(block, "seq", to_y)])
    pieces = []
    for k in range(4):
        part = permute(pair, "seq", functools.partial(to_x, k)) if k else pair
        pieces += [part, permute(part, "head", lambda i: i ^ 1)]
    return pieces


def add(a, b):
    return a.astype(F32) + b.astype(F32)


def local(
    latents,
    span_ids,
    patch_weight,
    patch_bias,
    norm_gain,
    query_weight,
    key_weight,
    value_weight,
    out_weight,
):
    seq = lax.axis_index("seq")
    frames = jnp.stack([seq, FRAMES - 1 - seq]).astype(jnp.int32)
    own_span = jnp.sum(jnp.where(frames[:, None] == jnp.arange(FRAMES)[None], span_ids[None], 0), axis=1)
    ends = jnp.sum((span_ids[None, :] <= own_span[:, None]).astype(jnp.int32), axis=1)
    head = lax.axis_index("head")
    places = jnp.stack([seq // 8, (seq // 4) % 2, head % 2, head // 2]).astype(jnp.int32)
    meta = jnp.concatenate([ends, frames, places])

    pieces = all_latents(latents)

    b0 = patch_bias.astype(BF16)
    b1 = (patch_bias - b0.astype(F32)).astype(BF16)
    b2 = (patch_bias - b0.astype(F32) - b1.astype(F32)).astype(BF16)
    rest = jnp.zeros((ROWS - 131, patch_bias.shape[0]), BF16)
    wide = jnp.concatenate([patch_weight, b0[None], b1[None], b2[None], rest], axis=0)
    parts = [wide] + [permute(wide, "head", lambda i, k=k: (i + k) % 4) for k in (1, 2, 3)]
    mg, mq, mv = through(parts, norm_gain, query_weight, key_weight, value_weight)

    w_t, _, _ = frequencies()
    spatial = spatial_angles()
    cs = jnp.asarray(np.tile(np.cos(spatial).T, (1, BF)), F32)
    ss = jnp.asarray(np.tile(np.sin(spatial).T, (1, BF)), F32)
    temporal = np.outer(np.arange(FRAMES), w_t)
    by_block = np.repeat(temporal.reshape(NB, BF, 16).transpose(0, 2, 1), FT, axis=2)
    ct = jnp.asarray(np.cos(by_block), F32)
    st = jnp.asarray(np.sin(by_block), F32)
    angle = frames.astype(F32)[:, None] * jnp.asarray(w_t, F32)[None]

    def of_queries(turn, space):
        own = jnp.broadcast_to(turn[:, None, :], (2, FT, 16))
        return jnp.concatenate([own, jnp.broadcast_to(jnp.asarray(space, F32)[None], (2, FT, 48))], axis=2) * SCALE

    cq = of_queries(jnp.cos(angle), np.cos(spatial))
    sq = of_queries(jnp.sin(angle), np.sin(spatial))
    cq = jnp.concatenate([cq, cq], axis=2)
    sq = jnp.concatenate([-sq, sq], axis=2)

    near, near_other, far, far_other, tokens = attention(
        meta, *pieces, mg, mq, mv, wide, cs, ss, ct, st, cq, sq, out_weight
    )
    swap = lambda x, bit: permute(x, "head", lambda i: i ^ bit)
    sent = swap(add(far, swap(far_other, 1)).astype(BF16), 2)
    kept = add(near, swap(near_other, 1)).astype(BF16)
    return (add(kept, sent) + tokens.astype(F32)).astype(BF16)


def solution(mesh):
    return jax.shard_map(
        local,
        mesh=mesh,
        in_specs=(
            P(None, "seq"),
            P(),
            P(None, "head"),
            P("head"),
            P(),
            P(None, "head"),
            P(None, "head"),
            P(None, "head"),
            P("head", None),
        ),
        out_specs=P("seq", "head"),
        check_vma=False,
    )
```

```python
import functools
import math

import jax
import jax.numpy as jnp
import numpy as np
from jax import lax
from jax.experimental import pallas as pl
from jax.experimental.pallas import tpu as pltpu
from jax.sharding import PartitionSpec as P

HD = 128
HEADS = 6
FT = 192
FRAMES = 64
BF = 4
BK = BF * FT
NB = FRAMES // BF
ROWS = 144
WIDTH = 24
EPS = 1e-06
YARN = 4.0
SCALE = (0.1 * math.log(YARN) + 1.0) ** 2 / math.sqrt(HD) * math.log2(math.e)
FAR = -1e30
LOW, HIGH = 2.0**-60, 2.0**100

F32 = jnp.float32
BF16 = jnp.bfloat16


def spectrum(count):
    return np.exp(-math.log(10000.0) * np.arange(count) / count)


def frequencies():
    pairs = HD // 2
    count_t, count_h = pairs // 4, 3 * pairs // 8
    base_t = spectrum(count_t)
    ramp = np.clip((FRAMES / 4.0 / (2.0 * math.pi / base_t) - 1.0) / 31.0, 0.0, 1.0)
    return base_t * (ramp + (1.0 - ramp) / YARN), spectrum(count_h), spectrum(pairs - count_t - count_h)


def spatial_angles():
    _, w_h, w_w = frequencies()
    inner = np.arange(FT)
    return np.concatenate(
        [np.outer(inner // WIDTH, w_h), np.outer(inner % WIDTH, w_w)], axis=1
    )


def dot(a, b):
    return jnp.dot(a, b, preferred_element_type=F32)


def kernel(
    meta,
    *refs,
):
    pieces, refs = refs[:8], refs[8:]
    (mg_ref, mq_ref, mv_ref, pw_ref, cs_ref, ss_ref, ct_ref, st_ref, cq_ref, sq_ref, wo_ref) = refs[:11]
    (outs, tokens_ref), refs = (refs[11:15], refs[15]), refs[16:]
    raw_ref, own_ref, q_ref, w_ref, u_ref, ho_ref, m_ref, k_ref, v_ref, res_ref, wide_ref, sems, out_sems, wide_sem = refs
    end_early, end_late = meta[0], meta[1]
    blocks_early = (end_early + BF - 1) // BF
    blocks_late = (end_late + BF - 1) // BF
    wide_copy = pltpu.make_async_copy(wo_ref, wide_ref, wide_sem)
    wide_copy.start()
    x_at, y_at, core, chip = meta[4], meta[5], meta[6], meta[7]

    copies = []
    for k in range(4):
        for c in range(2):
            rows = pl.ds(pl.multiple_of((core ^ c) * 32, 32), 32)
            for i in range(2):
                group = ((x_at + 4 - k) % 4) * 2 + (y_at ^ i)
                for late in range(2):
                    block = NB - 1 - group if late else group
                    copies.append(
                        pltpu.make_async_copy(
                            pieces[2 * k + c].at[i, late],
                            raw_ref.at[block, rows],
                            sems.at[len(copies)],
                        )
                    )
    for copy in copies:
        copy.start()
    for copy in copies:
        copy.wait()

    row = lax.broadcasted_iota(jnp.int32, (ROWS - 128, BK), 0)
    lane_frame = lax.broadcasted_iota(jnp.int32, (ROWS - 128, BK), 1) // FT
    ones = (row < 3).astype(F32).astype(BF16)

    def features(b):
        now = raw_ref[b]
        last = raw_ref[jnp.maximum(b - 1, 0)][:, BK - FT :]
        last = jnp.where(b > 0, last, jnp.zeros_like(last))
        before = jnp.concatenate([last, now[:, : BK - FT]], axis=1)
        return jnp.concatenate([before, now, ones], axis=0)

    def norm(x, gram):
        y = gram[:ROWS] + gram[ROWS:]
        return lax.rsqrt(jnp.sum(x.astype(F32) * y, axis=0, keepdims=True) + EPS)

    def scaled(x, r):
        tail = jnp.where(row == 0, r, jnp.where(row == 1, 1.0, 0.0))
        return jnp.concatenate([x[:128].astype(F32) * r, tail], axis=0).astype(BF16).T

    def prepare(b):
        inside = jnp.minimum(b, NB - 1)
        x = features(inside)
        big = dot(mg_ref[...], x)
        r = norm(x, big[HEADS * HD :])
        cos = jnp.concatenate([ct_ref[inside], cs_ref[...]], axis=0) * r
        sin = jnp.concatenate([st_ref[inside], ss_ref[...]], axis=0) * r
        cos, sin = cos.astype(BF16), sin.astype(BF16)
        end = jnp.where(row == 0, end_early, end_late)
        mask = jnp.where((row < 2) & (b * BF + lane_frame >= end), FAR, 0.0).astype(BF16)

        def keys(h):
            first, second = big[h * HD : h * HD + 64], big[h * HD + 64 : h * HD + HD]
            first, second = first.astype(BF16), second.astype(BF16)
            return jnp.concatenate(
                [
                    (first * cos - second * sin).astype(BF16),
                    (first * sin + second * cos).astype(BF16),
                    mask,
                ],
                axis=0,
            )

        return keys, lambda: scaled(x, r)

    for i in range(2):
        frame = meta[2 + i]
        rows = pl.ds(pl.multiple_of((frame % BF) * FT, FT), FT)
        x = features(frame // BF)
        own_ref[...] = x.T
        res_ref[4, pl.ds(i * FT, FT), :] = dot(own_ref[rows, :], pw_ref[...]).astype(BF16)
        own_ref[...] = scaled(x, norm(x, dot(mg_ref[HEADS * HD :], x)))
        own = own_ref[rows, :]
        lane = lax.broadcasted_iota(jnp.int32, (FT, ROWS - 128), 1)
        select = (lane == i).astype(F32).astype(BF16)
        for h in range(HEADS):
            pre = dot(own, mq_ref[:, pl.ds(h * HD, HD)])
            rotated = pre * cq_ref[i] + pltpu.roll(pre, 64, 1) * sq_ref[i]
            q_ref[i, h] = jnp.concatenate([rotated.astype(BF16), select], axis=1)

    tokens_copy = pltpu.make_async_copy(res_ref.at[4], tokens_ref, out_sems.at[4])
    tokens_copy.start()
    u_ref[...] = jnp.zeros_like(u_ref)

    def fill(b):
        keys, values = prepare(b)
        for h in range(HEADS):
            k_ref[h] = keys(h)
        v_ref[...] = values()

    def visit(frames, b, carry):
        keys, values = prepare(b + 1)
        for h in range(HEADS):
            q = jnp.concatenate([q_ref[i, h] for i in frames], axis=0)
            w = jnp.exp2(dot(q, k_ref[h])).astype(BF16)
            k_ref[h] = keys(h)
            for n, i in enumerate(frames):
                w_ref[i, pl.ds(h * FT, FT)] = w[n * FT : (n + 1) * FT]
        for i in frames:
            u_ref[i] += dot(w_ref[i], v_ref[...])
        v_ref[...] = values()
        return carry

    fill(0)
    lax.fori_loop(0, blocks_early, functools.partial(visit, (0, 1)), 0)
    lax.fori_loop(blocks_early, blocks_late, functools.partial(visit, (1,)), 0)

    total = u_ref[:, :, 129:130]
    good = jnp.where((total >= LOW) & (total <= HIGH), 1.0, 0.0)
    bad = jnp.min(good) < 0.5

    @pl.when(bad)
    def _():
        u_ref[...] = jnp.zeros_like(u_ref)
        m_ref[...] = jnp.full_like(m_ref, FAR)

        def visit_again(b, carry):
            fill(b)
            for h in range(HEADS):
                k = k_ref[h]
                rows = pl.ds(h * FT, FT)
                for i in range(2):
                    s = dot(q_ref[i, h], k)
                    old = m_ref[i, rows]
                    new = jnp.maximum(old, jnp.max(s, axis=1, keepdims=True))
                    w = jnp.exp2(s - new).astype(BF16)
                    u_ref[i, rows] = u_ref[i, rows] * jnp.exp2(old - new) + dot(w, v_ref[...])
                    m_ref[i, rows] = new
            return carry

        lax.fori_loop(0, blocks_late, visit_again, 0)

    for i in range(2):
        for h in range(HEADS):
            u = u_ref[i, pl.ds(h * FT, FT)]
            mixed = (u / u[:, 129:130]).astype(BF16)
            ho_ref[pl.ds(i * FT, FT), pl.ds(h * HD, HD)] = dot(
                mixed, mv_ref[:, pl.ds(h * HD, HD)]
            ).astype(BF16)
    sent = [tokens_copy]
    wide_copy.wait()
    for n in (3, 2, 1, 0):
        group = (chip ^ (n // 2)) * 2 + (core ^ (n % 2))
        columns = pl.ds(pl.multiple_of(group * 768, 768), 768)
        res_ref[n] = dot(ho_ref[...], wide_ref[:, columns]).astype(BF16)
        sent.append(pltpu.make_async_copy(res_ref.at[n], outs[n], out_sems.at[n]))
        sent[-1].start()
    for copy in sent:
        copy.wait()


def attention(meta, *arrays):
    vmem = pl.BlockSpec(memory_space=pltpu.VMEM)
    hbm = pl.BlockSpec(memory_space=pl.ANY)
    shape = jax.ShapeDtypeStruct((2 * FT, 768), BF16)
    return pl.pallas_call(
        kernel,
        in_specs=[pl.BlockSpec(memory_space=pltpu.SMEM)] + [hbm] * 8 + [vmem] * 10 + [hbm],
        out_specs=(hbm,) * 5,
        out_shape=(shape,) * 5,
        scratch_shapes=[
            pltpu.VMEM((NB, 64, BK), BF16),
            pltpu.VMEM((BK, ROWS), BF16),
            pltpu.VMEM((2, HEADS, FT, ROWS), BF16),
            pltpu.VMEM((2, HEADS * FT, BK), BF16),
            pltpu.VMEM((2, HEADS * FT, ROWS), F32),
            pltpu.VMEM((2 * FT, HEADS * HD), BF16),
            pltpu.VMEM((2, HEADS * FT, 1), F32),
            pltpu.VMEM((HEADS, ROWS, BK), BF16),
            pltpu.VMEM((BK, ROWS), BF16),
            pltpu.VMEM((5, 2 * FT, HEADS * HD), BF16),
            pltpu.VMEM((HEADS * HD, 4 * HEADS * HD), BF16),
            pltpu.SemaphoreType.DMA((32,)),
            pltpu.SemaphoreType.DMA((5,)),
            pltpu.SemaphoreType.DMA,
        ],
        compiler_params=pltpu.CompilerParams(vmem_limit_bytes=52 * 2**20),
    )(meta, *arrays)


def permute(x, axis, to):
    return lax.ppermute(x, axis, [(i, to(i)) for i in range(lax.axis_size(axis))])


def weights_kernel(me, p0, p1, p2, p3, gain, wq, wk, wv, mg_ref, mq_ref, mv_ref, aq, ak, av, ag):
    k = pl.program_id(0)

    @pl.when(k == 0)
    def _():
        for ref in (aq, ak, av, ag):
            ref[...] = jnp.zeros_like(ref)

    part = jnp.where(k < 2, jnp.where(k == 0, p0[...], p1[...]), jnp.where(k == 2, p2[...], p3[...]))
    wide = part.astype(F32)
    bias = wide[128:129] + wide[129:130] + wide[130:131]
    row = lax.broadcasted_iota(jnp.int32, (ROWS - 128, part.shape[1]), 0)
    gained = jnp.concatenate([wide[:128], jnp.where(row == 0, bias, 0.0)], axis=0) * gain[0]
    gained = gained.astype(BF16)
    aq[...] += dot(gained, wq[...])
    ak[...] += dot(gained, wk[...])
    av[...] += dot(gained, wv[...])
    ag[...] += lax.dot_general(part, part, (((1,), (1,)), ((), ())), preferred_element_type=F32)

    @pl.when(k == 3)
    def _():
        mq_ref[...] = aq[...].astype(BF16)
        mv_ref[...] = av[...].astype(BF16)
        mg_ref[: HEADS * HD, :] = ak[...].T.astype(BF16)
        gram = ag[...] * (1.0 / (4 * part.shape[1]))
        high = gram.astype(BF16)
        mg_ref[HEADS * HD : HEADS * HD + ROWS, :] = high
        mg_ref[HEADS * HD + ROWS :, :] = (gram - high.astype(F32)).astype(BF16)


def through(parts, gain, wq, wk, wv):
    columns = HEADS * HD
    whole = lambda *shape: pl.BlockSpec(shape, lambda k, me: (0,) * len(shape))
    source = lambda k, me: (me[0] + 4 - k) % 4
    weight = pl.BlockSpec((columns, columns), lambda k, me: (source(k, me), 0))
    return pl.pallas_call(
        weights_kernel,
        grid_spec=pltpu.PrefetchScalarGridSpec(
            num_scalar_prefetch=1,
            grid=(4,),
            in_specs=[whole(ROWS, columns)] * 4
            + [pl.BlockSpec((1, 1, columns), lambda k, me: (source(k, me), 0, 0))]
            + [weight] * 3,
            out_specs=[
                whole(columns + 2 * ROWS, ROWS),
                whole(ROWS, columns),
                whole(ROWS, columns),
            ],
            scratch_shapes=[pltpu.VMEM((ROWS, columns), F32)] * 3 + [pltpu.VMEM((ROWS, ROWS), F32)],
        ),
        out_shape=[
            jax.ShapeDtypeStruct((columns + 2 * ROWS, ROWS), BF16),
            jax.ShapeDtypeStruct((ROWS, columns), BF16),
            jax.ShapeDtypeStruct((ROWS, columns), BF16),
        ],
        compiler_params=pltpu.CompilerParams(vmem_limit_bytes=57 * 2**20),
        cost_estimate=pl.CostEstimate(
            flops=2 * ROWS * 3072 * 2400, bytes_accessed=3 * 3072 * 768 * 2, transcendentals=0
        ),
    )(lax.axis_index("head").astype(jnp.int32).reshape(1), *parts, gain.reshape(4, 1, columns), wq, wk, wv)


def join_kernel(z, p0, p1, p2, p3, out):
    for place in range(4):
        k = (z[0] + 4 - place) % 4
        part = jnp.where(k < 2, jnp.where(k == 0, p0[...], p1[...]), jnp.where(k == 2, p2[...], p3[...]))
        out[0, :, place * FT : (place + 1) * FT] = part[:, :FT]
        out[1, :, (3 - place) * FT : (4 - place) * FT] = part[:, FT:]


def join(z, parts):
    vmem = pl.BlockSpec(memory_space=pltpu.VMEM)
    return pl.pallas_call(
        join_kernel,
        in_specs=[pl.BlockSpec(memory_space=pltpu.SMEM)] + [vmem] * 4,
        out_specs=vmem,
        out_shape=jax.ShapeDtypeStruct((2, 32, BK), BF16),
        compiler_params=pltpu.CompilerParams(vmem_limit_bytes=2 * 2**20),
        cost_estimate=pl.CostEstimate(flops=0, bytes_accessed=200000, transcendentals=0),
    )(z.astype(jnp.int32).reshape(1), *parts)


def all_latents(latents):
    seq, core = lax.axis_index("seq"), lax.axis_index("head") % 2

    def place(i):
        return i // 8, (i // 4) % 2, i % 4

    def at(x, y, z):
        return (x * 2 + y) * 4 + z

    def to_y(i):
        x, y, z = place(i)
        return at(x, 1 - y, z)

    def to_z(k, i):
        x, y, z = place(i)
        return at(x, y, (z + k) % 4)

    def to_x(k, i):
        x, y, z = place(i)
        return at((x + k) % 4, y, z)

    half = lax.dynamic_slice_in_dim(latents, core * 32, 32, 0)
    parts = [half] + [permute(half, "seq", functools.partial(to_z, k)) for k in (1, 2, 3)]
    block = join(seq % 4, parts)
    pair = jnp.stack([block, permute(block, "seq", to_y)])
    pieces = []
    for k in range(4):
        part = permute(pair, "seq", functools.partial(to_x, k)) if k else pair
        pieces += [part, permute(part, "head", lambda i: i ^ 1)]
    return pieces


def add(a, b):
    return a.astype(F32) + b.astype(F32)


def local(
    latents,
    span_ids,
    patch_weight,
    patch_bias,
    norm_gain,
    query_weight,
    key_weight,
    value_weight,
    out_weight,
):
    seq = lax.axis_index("seq")
    frames = jnp.stack([seq, FRAMES - 1 - seq]).astype(jnp.int32)
    own_span = jnp.sum(jnp.where(frames[:, None] == jnp.arange(FRAMES)[None], span_ids[None], 0), axis=1)
    ends = jnp.sum((span_ids[None, :] <= own_span[:, None]).astype(jnp.int32), axis=1)
    head = lax.axis_index("head")
    places = jnp.stack([seq // 8, (seq // 4) % 2, head % 2, head // 2]).astype(jnp.int32)
    meta = jnp.concatenate([ends, frames, places])

    pieces = all_latents(latents)

    b0 = patch_bias.astype(BF16)
    b1 = (patch_bias - b0.astype(F32)).astype(BF16)
    b2 = (patch_bias - b0.astype(F32) - b1.astype(F32)).astype(BF16)
    rest = jnp.zeros((ROWS - 131, patch_bias.shape[0]), BF16)
    wide = jnp.concatenate([patch_weight, b0[None], b1[None], b2[None], rest], axis=0)
    parts = [wide] + [permute(wide, "head", lambda i, k=k: (i + k) % 4) for k in (1, 2, 3)]
    mg, mq, mv = through(parts, norm_gain, query_weight, key_weight, value_weight)

    w_t, _, _ = frequencies()
    spatial = spatial_angles()
    cs = jnp.asarray(np.tile(np.cos(spatial).T, (1, BF)), F32)
    ss = jnp.asarray(np.tile(np.sin(spatial).T, (1, BF)), F32)
    temporal = np.outer(np.arange(FRAMES), w_t)
    by_block = np.repeat(temporal.reshape(NB, BF, 16).transpose(0, 2, 1), FT, axis=2)
    ct = jnp.asarray(np.cos(by_block), F32)
    st = jnp.asarray(np.sin(by_block), F32)
    angle = frames.astype(F32)[:, None] * jnp.asarray(w_t, F32)[None]

    def of_queries(turn, space):
        own = jnp.broadcast_to(turn[:, None, :], (2, FT, 16))
        return jnp.concatenate([own, jnp.broadcast_to(jnp.asarray(space, F32)[None], (2, FT, 48))], axis=2) * SCALE

    cq = of_queries(jnp.cos(angle), np.cos(spatial))
    sq = of_queries(jnp.sin(angle), np.sin(spatial))
    cq = jnp.concatenate([cq, cq], axis=2)
    sq = jnp.concatenate([-sq, sq], axis=2)

    near, near_other, far, far_other, tokens = attention(
        meta, *pieces, mg, mq, mv, wide, cs, ss, ct, st, cq, sq, out_weight
    )
    swap = lambda x, bit: permute(x, "head", lambda i: i ^ bit)
    sent = swap(add(far, swap(far_other, 1)).astype(BF16), 2)
    kept = add(near, swap(near_other, 1)).astype(BF16)
    return (add(kept, sent) + tokens.astype(F32)).astype(BF16)


def solution(mesh):
    return jax.shard_map(
        local,
        mesh=mesh,
        in_specs=(
            P(None, "seq"),
            P(),
            P(None, "head"),
            P("head"),
            P(),
            P(None, "head"),
            P(None, "head"),
            P(None, "head"),
            P("head", None),
        ),
        out_specs=P("seq", "head"),
        check_vma=False,
    )
```

```python
import functools
import math

import jax
import jax.numpy as jnp
import numpy as np
from jax import lax
from jax.experimental import pallas as pl
from jax.experimental.pallas import tpu as pltpu
from jax.sharding import PartitionSpec as P

HD = 128
HEADS = 6
FT = 192
FRAMES = 64
BF = 4
BK = BF * FT
NB = FRAMES // BF
ROWS = 144
WIDTH = 24
EPS = 1e-06
YARN = 4.0
SCALE = (0.1 * math.log(YARN) + 1.0) ** 2 / math.sqrt(HD) * math.log2(math.e)
FAR = -1e30
LOW, HIGH = 2.0**-60, 2.0**100

F32 = jnp.float32
BF16 = jnp.bfloat16


def spectrum(count):
    return np.exp(-math.log(10000.0) * np.arange(count) / count)


def frequencies():
    pairs = HD // 2
    count_t, count_h = pairs // 4, 3 * pairs // 8
    base_t = spectrum(count_t)
    ramp = np.clip((FRAMES / 4.0 / (2.0 * math.pi / base_t) - 1.0) / 31.0, 0.0, 1.0)
    return base_t * (ramp + (1.0 - ramp) / YARN), spectrum(count_h), spectrum(pairs - count_t - count_h)


def spatial_angles():
    _, w_h, w_w = frequencies()
    inner = np.arange(FT)
    return np.concatenate(
        [np.outer(inner // WIDTH, w_h), np.outer(inner % WIDTH, w_w)], axis=1
    )


def dot(a, b):
    return jnp.dot(a, b, preferred_element_type=F32)


def kernel(
    meta,
    *refs,
):
    pieces, refs = refs[:8], refs[8:]
    (mg_ref, mq_ref, mv_ref, pw_ref, cs_ref, ss_ref, ct_ref, st_ref, cq_ref, sq_ref, wo_ref) = refs[:11]
    (outs, tokens_ref), refs = (refs[11:15], refs[15]), refs[16:]
    raw_ref, own_ref, q_ref, w_ref, u_ref, ho_ref, m_ref, k_ref, v_ref, res_ref, wide_ref, sems, out_sems, wide_sem = refs
    end_early, end_late = meta[0], meta[1]
    blocks_early = (end_early + BF - 1) // BF
    blocks_late = (end_late + BF - 1) // BF
    wide_copy = pltpu.make_async_copy(wo_ref, wide_ref, wide_sem)
    wide_copy.start()
    x_at, y_at, core, chip = meta[4], meta[5], meta[6], meta[7]

    copies = []
    for k in range(4):
        for c in range(2):
            rows = pl.ds(pl.multiple_of((core ^ c) * 32, 32), 32)
            for i in range(2):
                group = ((x_at + 4 - k) % 4) * 2 + (y_at ^ i)
                for late in range(2):
                    block = NB - 1 - group if late else group
                    copies.append(
                        pltpu.make_async_copy(
                            pieces[2 * k + c].at[i, late],
                            raw_ref.at[block, rows],
                            sems.at[len(copies)],
                        )
                    )
    for copy in copies:
        copy.start()
    for copy in copies:
        copy.wait()

    row = lax.broadcasted_iota(jnp.int32, (ROWS - 128, BK), 0)
    lane_frame = lax.broadcasted_iota(jnp.int32, (ROWS - 128, BK), 1) // FT
    ones = (row < 3).astype(F32).astype(BF16)

    def features(b):
        now = raw_ref[b]
        last = raw_ref[jnp.maximum(b - 1, 0)][:, BK - FT :]
        last = jnp.where(b > 0, last, jnp.zeros_like(last))
        before = jnp.concatenate([last, now[:, : BK - FT]], axis=1)
        return jnp.concatenate([before, now, ones], axis=0)

    def norm(x, gram):
        y = gram[:ROWS] + gram[ROWS:]
        return lax.rsqrt(jnp.sum(x.astype(F32) * y, axis=0, keepdims=True) + EPS)

    def scaled(x, r):
        tail = jnp.where(row == 0, r, jnp.where(row == 1, 1.0, 0.0))
        return jnp.concatenate([x[:128].astype(F32) * r, tail], axis=0).astype(BF16).T

    def prepare(b):
        inside = jnp.minimum(b, NB - 1)
        x = features(inside)
        big = dot(mg_ref[...], x)
        r = norm(x, big[HEADS * HD :])
        cos = jnp.concatenate([ct_ref[inside], cs_ref[...]], axis=0) * r
        sin = jnp.concatenate([st_ref[inside], ss_ref[...]], axis=0) * r
        cos, sin = cos.astype(BF16), sin.astype(BF16)
        end = jnp.where(row == 0, end_early, end_late)
        mask = jnp.where((row < 2) & (b * BF + lane_frame >= end), FAR, 0.0).astype(BF16)

        def keys(h):
            first, second = big[h * HD : h * HD + 64], big[h * HD + 64 : h * HD + HD]
            first, second = first.astype(BF16), second.astype(BF16)
            return jnp.concatenate(
                [
                    (first * cos - second * sin).astype(BF16),
                    (first * sin + second * cos).astype(BF16),
                    mask,
                ],
                axis=0,
            )

        return keys, lambda: scaled(x, r)

    for i in range(2):
        frame = meta[2 + i]
        rows = pl.ds(pl.multiple_of((frame % BF) * FT, FT), FT)
        x = features(frame // BF)
        own_ref[...] = x.T
        res_ref[4, pl.ds(i * FT, FT), :] = dot(own_ref[rows, :], pw_ref[...]).astype(BF16)
        own_ref[...] = scaled(x, norm(x, dot(mg_ref[HEADS * HD :], x)))
        own = own_ref[rows, :]
        lane = lax.broadcasted_iota(jnp.int32, (FT, ROWS - 128), 1)
        select = (lane == i).astype(F32).astype(BF16)
        for h in range(HEADS):
            pre = dot(own, mq_ref[:, pl.ds(h * HD, HD)])
            rotated = pre * cq_ref[i] + pltpu.roll(pre, 64, 1) * sq_ref[i]
            q_ref[i, h] = jnp.concatenate([rotated.astype(BF16), select], axis=1)

    tokens_copy = pltpu.make_async_copy(res_ref.at[4], tokens_ref, out_sems.at[4])
    tokens_copy.start()
    u_ref[...] = jnp.zeros_like(u_ref)

    def fill(b):
        keys, values = prepare(b)
        for h in range(HEADS):
            k_ref[h] = keys(h)
        v_ref[...] = values()

    def visit(frames, b, carry):
        keys, values = prepare(b + 1)
        for h in range(HEADS):
            q = jnp.concatenate([q_ref[i, h] for i in frames], axis=0)
            w = jnp.exp2(dot(q, k_ref[h])).astype(BF16)
            k_ref[h] = keys(h)
            for n, i in enumerate(frames):
                w_ref[i, pl.ds(h * FT, FT)] = w[n * FT : (n + 1) * FT]
        for i in frames:
            u_ref[i] += dot(w_ref[i], v_ref[...])
        v_ref[...] = values()
        return carry

    fill(0)
    lax.fori_loop(0, blocks_early, functools.partial(visit, (0, 1)), 0)
    lax.fori_loop(blocks_early, blocks_late, functools.partial(visit, (1,)), 0)

    total = u_ref[:, :, 129:130]
    good = jnp.where((total >= LOW) & (total <= HIGH), 1.0, 0.0)
    bad = jnp.min(good) < 0.5

    @pl.when(bad)
    def _():
        u_ref[...] = jnp.zeros_like(u_ref)
        m_ref[...] = jnp.full_like(m_ref, FAR)

        def visit_again(b, carry):
            fill(b)
            for h in range(HEADS):
                k = k_ref[h]
                rows = pl.ds(h * FT, FT)
                for i in range(2):
                    s = dot(q_ref[i, h], k)
                    old = m_ref[i, rows]
                    new = jnp.maximum(old, jnp.max(s, axis=1, keepdims=True))
                    w = jnp.exp2(s - new).astype(BF16)
                    u_ref[i, rows] = u_ref[i, rows] * jnp.exp2(old - new) + dot(w, v_ref[...])
                    m_ref[i, rows] = new
            return carry

        lax.fori_loop(0, blocks_late, visit_again, 0)

    for i in range(2):
        for h in range(HEADS):
            u = u_ref[i, pl.ds(h * FT, FT)]
            mixed = (u / u[:, 129:130]).astype(BF16)
            ho_ref[pl.ds(i * FT, FT), pl.ds(h * HD, HD)] = dot(
                mixed, mv_ref[:, pl.ds(h * HD, HD)]
            ).astype(BF16)
    sent = [tokens_copy]
    wide_copy.wait()
    for n in (3, 2, 1, 0):
        group = (chip ^ (n // 2)) * 2 + (core ^ (n % 2))
        columns = pl.ds(pl.multiple_of(group * 768, 768), 768)
        res_ref[n] = dot(ho_ref[...], wide_ref[:, columns]).astype(BF16)
        sent.append(pltpu.make_async_copy(res_ref.at[n], outs[n], out_sems.at[n]))
        sent[-1].start()
    for copy in sent:
        copy.wait()


def attention(meta, *arrays):
    vmem = pl.BlockSpec(memory_space=pltpu.VMEM)
    hbm = pl.BlockSpec(memory_space=pl.ANY)
    shape = jax.ShapeDtypeStruct((2 * FT, 768), BF16)
    return pl.pallas_call(
        kernel,
        in_specs=[pl.BlockSpec(memory_space=pltpu.SMEM)] + [hbm] * 8 + [vmem] * 10 + [hbm],
        out_specs=(hbm,) * 5,
        out_shape=(shape,) * 5,
        scratch_shapes=[
            pltpu.VMEM((NB, 64, BK), BF16),
            pltpu.VMEM((BK, ROWS), BF16),
            pltpu.VMEM((2, HEADS, FT, ROWS), BF16),
            pltpu.VMEM((2, HEADS * FT, BK), BF16),
            pltpu.VMEM((2, HEADS * FT, ROWS), F32),
            pltpu.VMEM((2 * FT, HEADS * HD), BF16),
            pltpu.VMEM((2, HEADS * FT, 1), F32),
            pltpu.VMEM((HEADS, ROWS, BK), BF16),
            pltpu.VMEM((BK, ROWS), BF16),
            pltpu.VMEM((5, 2 * FT, HEADS * HD), BF16),
            pltpu.VMEM((HEADS * HD, 4 * HEADS * HD), BF16),
            pltpu.SemaphoreType.DMA((32,)),
            pltpu.SemaphoreType.DMA((5,)),
            pltpu.SemaphoreType.DMA,
        ],
        compiler_params=pltpu.CompilerParams(vmem_limit_bytes=52 * 2**20),
    )(meta, *arrays)


def permute(x, axis, to):
    return lax.ppermute(x, axis, [(i, to(i)) for i in range(lax.axis_size(axis))])


def weights_kernel(me, p0, p1, p2, p3, gain, wq, wk, wv, mg_ref, mq_ref, mv_ref, aq, ak, av, ag):
    k = pl.program_id(0)

    @pl.when(k == 0)
    def _():
        for ref in (aq, ak, av, ag):
            ref[...] = jnp.zeros_like(ref)

    part = jnp.where(k < 2, jnp.where(k == 0, p0[...], p1[...]), jnp.where(k == 2, p2[...], p3[...]))
    wide = part.astype(F32)
    bias = wide[128:129] + wide[129:130] + wide[130:131]
    row = lax.broadcasted_iota(jnp.int32, (ROWS - 128, part.shape[1]), 0)
    gained = jnp.concatenate([wide[:128], jnp.where(row == 0, bias, 0.0)], axis=0) * gain[0]
    gained = gained.astype(BF16)
    aq[...] += dot(gained, wq[...])
    ak[...] += dot(gained, wk[...])
    av[...] += dot(gained, wv[...])
    ag[...] += lax.dot_general(part, part, (((1,), (1,)), ((), ())), preferred_element_type=F32)

    @pl.when(k == 3)
    def _():
        mq_ref[...] = aq[...].astype(BF16)
        mv_ref[...] = av[...].astype(BF16)
        mg_ref[: HEADS * HD, :] = ak[...].T.astype(BF16)
        gram = ag[...] * (1.0 / (4 * part.shape[1]))
        high = gram.astype(BF16)
        mg_ref[HEADS * HD : HEADS * HD + ROWS, :] = high
        mg_ref[HEADS * HD + ROWS :, :] = (gram - high.astype(F32)).astype(BF16)


def through(parts, gain, wq, wk, wv):
    columns = HEADS * HD
    whole = lambda *shape: pl.BlockSpec(shape, lambda k, me: (0,) * len(shape))
    source = lambda k, me: me[0] ^ k
    weight = pl.BlockSpec((columns, columns), lambda k, me: (source(k, me), 0))
    return pl.pallas_call(
        weights_kernel,
        grid_spec=pltpu.PrefetchScalarGridSpec(
            num_scalar_prefetch=1,
            grid=(4,),
            in_specs=[whole(ROWS, columns)] * 4
            + [pl.BlockSpec((1, 1, columns), lambda k, me: (source(k, me), 0, 0))]
            + [weight] * 3,
            out_specs=[
                whole(columns + 2 * ROWS, ROWS),
                whole(ROWS, columns),
                whole(ROWS, columns),
            ],
            scratch_shapes=[pltpu.VMEM((ROWS, columns), F32)] * 3 + [pltpu.VMEM((ROWS, ROWS), F32)],
        ),
        out_shape=[
            jax.ShapeDtypeStruct((columns + 2 * ROWS, ROWS), BF16),
            jax.ShapeDtypeStruct((ROWS, columns), BF16),
            jax.ShapeDtypeStruct((ROWS, columns), BF16),
        ],
        compiler_params=pltpu.CompilerParams(vmem_limit_bytes=57 * 2**20),
        cost_estimate=pl.CostEstimate(
            flops=2 * ROWS * 3072 * 2400, bytes_accessed=3 * 3072 * 768 * 2, transcendentals=0
        ),
    )(lax.axis_index("head").astype(jnp.int32).reshape(1), *parts, gain.reshape(4, 1, columns), wq, wk, wv)


def join_kernel(z, p0, p1, p2, p3, out):
    for place in range(4):
        k = (z[0] + 4 - place) % 4
        part = jnp.where(k < 2, jnp.where(k == 0, p0[...], p1[...]), jnp.where(k == 2, p2[...], p3[...]))
        out[0, :, place * FT : (place + 1) * FT] = part[:, :FT]
        out[1, :, (3 - place) * FT : (4 - place) * FT] = part[:, FT:]


def join(z, parts):
    vmem = pl.BlockSpec(memory_space=pltpu.VMEM)
    return pl.pallas_call(
        join_kernel,
        in_specs=[pl.BlockSpec(memory_space=pltpu.SMEM)] + [vmem] * 4,
        out_specs=vmem,
        out_shape=jax.ShapeDtypeStruct((2, 32, BK), BF16),
        compiler_params=pltpu.CompilerParams(vmem_limit_bytes=2 * 2**20),
        cost_estimate=pl.CostEstimate(flops=0, bytes_accessed=200000, transcendentals=0),
    )(z.astype(jnp.int32).reshape(1), *parts)


def all_latents(latents):
    seq, core = lax.axis_index("seq"), lax.axis_index("head") % 2

    def place(i):
        return i // 8, (i // 4) % 2, i % 4

    def at(x, y, z):
        return (x * 2 + y) * 4 + z

    def to_y(i):
        x, y, z = place(i)
        return at(x, 1 - y, z)

    def to_z(k, i):
        x, y, z = place(i)
        return at(x, y, (z + k) % 4)

    def to_x(k, i):
        x, y, z = place(i)
        return at((x + k) % 4, y, z)

    half = lax.dynamic_slice_in_dim(latents, core * 32, 32, 0)
    parts = [half] + [permute(half, "seq", functools.partial(to_z, k)) for k in (1, 2, 3)]
    block = join(seq % 4, parts)
    pair = jnp.stack([block, permute(block, "seq", to_y)])
    return [pair] + [permute(pair, "seq", functools.partial(to_x, k)) for k in (1, 2, 3)]


def swap(x, bit):
    return permute(x, "head", lambda i: i ^ bit)


def add(a, b):
    return a.astype(F32) + b.astype(F32)


def local(
    latents,
    span_ids,
    patch_weight,
    patch_bias,
    norm_gain,
    query_weight,
    key_weight,
    value_weight,
    out_weight,
):
    seq = lax.axis_index("seq")
    frames = jnp.stack([seq, FRAMES - 1 - seq]).astype(jnp.int32)
    own_span = jnp.sum(jnp.where(frames[:, None] == jnp.arange(FRAMES)[None], span_ids[None], 0), axis=1)
    ends = jnp.sum((span_ids[None, :] <= own_span[:, None]).astype(jnp.int32), axis=1)
    head = lax.axis_index("head")
    places = jnp.stack([seq // 8, (seq // 4) % 2, head % 2, head // 2]).astype(jnp.int32)
    meta = jnp.concatenate([ends, frames, places])

    halves = all_latents(latents)

    b0 = patch_bias.astype(BF16)
    b1 = (patch_bias - b0.astype(F32)).astype(BF16)
    b2 = (patch_bias - b0.astype(F32) - b1.astype(F32)).astype(BF16)
    rest = jnp.zeros((ROWS - 131, patch_bias.shape[0]), BF16)
    wide = jnp.concatenate([patch_weight, b0[None], b1[None], b2[None], rest], axis=0)
    far_part = swap(wide, 2)
    parts = [wide, swap(wide, 1), far_part, swap(far_part, 1)]
    mg, mq, mv = through(parts, norm_gain, query_weight, key_weight, value_weight)
    others = [swap(halves[0], 1)] + [
        swap(lax.optimization_barrier((part, mq))[0], 1) for part in halves[1:]
    ]
    pieces = [piece for pair in zip(halves, others) for piece in pair]

    w_t, _, _ = frequencies()
    spatial = spatial_angles()
    cs = jnp.asarray(np.tile(np.cos(spatial).T, (1, BF)), F32)
    ss = jnp.asarray(np.tile(np.sin(spatial).T, (1, BF)), F32)
    temporal = np.outer(np.arange(FRAMES), w_t)
    by_block = np.repeat(temporal.reshape(NB, BF, 16).transpose(0, 2, 1), FT, axis=2)
    ct = jnp.asarray(np.cos(by_block), F32)
    st = jnp.asarray(np.sin(by_block), F32)
    angle = frames.astype(F32)[:, None] * jnp.asarray(w_t, F32)[None]

    def of_queries(turn, space):
        own = jnp.broadcast_to(turn[:, None, :], (2, FT, 16))
        return jnp.concatenate([own, jnp.broadcast_to(jnp.asarray(space, F32)[None], (2, FT, 48))], axis=2) * SCALE

    cq = of_queries(jnp.cos(angle), np.cos(spatial))
    sq = of_queries(jnp.sin(angle), np.sin(spatial))
    cq = jnp.concatenate([cq, cq], axis=2)
    sq = jnp.concatenate([-sq, sq], axis=2)

    near, near_other, far, far_other, tokens = attention(
        meta, *pieces, mg, mq, mv, wide, cs, ss, ct, st, cq, sq, out_weight
    )
    sent = swap(add(far, swap(far_other, 1)).astype(BF16), 2)
    kept = add(near, swap(near_other, 1)).astype(BF16)
    return (add(kept, sent) + tokens.astype(F32)).astype(BF16)


def solution(mesh):
    return jax.shard_map(
        local,
        mesh=mesh,
        in_specs=(
            P(None, "seq"),
            P(),
            P(None, "head"),
            P("head"),
            P(),
            P(None, "head"),
            P(None, "head"),
            P(None, "head"),
            P("head", None),
        ),
        out_specs=P("seq", "head"),
        check_vma=False,
    )
```

```python
import functools
import math

import jax
import jax.numpy as jnp
import numpy as np
from jax import lax
from jax.experimental import pallas as pl
from jax.experimental.pallas import tpu as pltpu
from jax.sharding import PartitionSpec as P

HD = 128
HEADS = 6
FT = 192
FRAMES = 64
BF = 4
BK = BF * FT
NB = FRAMES // BF
ROWS = 144
WIDTH = 24
EPS = 1e-06
YARN = 4.0
SCALE = (0.1 * math.log(YARN) + 1.0) ** 2 / math.sqrt(HD) * math.log2(math.e)
FAR = -1e30
LOW, HIGH = 2.0**-60, 2.0**100

F32 = jnp.float32
BF16 = jnp.bfloat16


def spectrum(count):
    return np.exp(-math.log(10000.0) * np.arange(count) / count)


def frequencies():
    pairs = HD // 2
    count_t, count_h = pairs // 4, 3 * pairs // 8
    base_t = spectrum(count_t)
    ramp = np.clip((FRAMES / 4.0 / (2.0 * math.pi / base_t) - 1.0) / 31.0, 0.0, 1.0)
    return base_t * (ramp + (1.0 - ramp) / YARN), spectrum(count_h), spectrum(pairs - count_t - count_h)


def spatial_angles():
    _, w_h, w_w = frequencies()
    inner = np.arange(FT)
    return np.concatenate(
        [np.outer(inner // WIDTH, w_h), np.outer(inner % WIDTH, w_w)], axis=1
    )


def dot(a, b):
    return jnp.dot(a, b, preferred_element_type=F32)


def kernel(seq_ref, head_ref, span_ref, *refs):
    pieces, refs = refs[:8], refs[8:]
    (mg_ref, mq_ref, mv_ref, pw_ref, cs_ref, ss_ref, ct_ref, st_ref, cq_ref, sq_ref, tq_ref, wo_ref) = refs[:12]
    (outs, tokens_ref), refs = (refs[12:16], refs[16]), refs[17:]
    raw_ref, own_ref, q_ref, w_ref, u_ref, ho_ref, m_ref, k_ref, v_ref, res_ref, wide_ref, sems, out_sems, wide_sem = refs
    seq, head = seq_ref[0], head_ref[0]
    own_frames = (seq, FRAMES - 1 - seq)

    def end_of(frame):
        count = lambda g, seen: seen + (span_ref[g] <= span_ref[frame]).astype(jnp.int32)
        return lax.fori_loop(0, FRAMES, count, 0)

    end_early, end_late = end_of(own_frames[0]), end_of(own_frames[1])
    blocks_early = (end_early + BF - 1) // BF
    blocks_late = (end_late + BF - 1) // BF
    wide_copy = pltpu.make_async_copy(wo_ref, wide_ref, wide_sem)
    wide_copy.start()
    x_at, y_at, core, chip = seq // 8, (seq // 4) % 2, head % 2, head // 2

    copies = []
    for k in range(4):
        for c in range(2):
            rows = pl.ds(pl.multiple_of((core ^ c) * 32, 32), 32)
            for i in range(2):
                group = ((x_at + 4 - k) % 4) * 2 + (y_at ^ i)
                for late in range(2):
                    block = NB - 1 - group if late else group
                    copies.append(
                        pltpu.make_async_copy(
                            pieces[2 * k + c].at[i, late],
                            raw_ref.at[block, rows],
                            sems.at[len(copies)],
                        )
                    )
    for copy in copies:
        copy.start()
    for copy in copies:
        copy.wait()

    row = lax.broadcasted_iota(jnp.int32, (ROWS - 128, BK), 0)
    lane_frame = lax.broadcasted_iota(jnp.int32, (ROWS - 128, BK), 1) // FT
    ones = (row < 3).astype(F32).astype(BF16)

    def features(b):
        now = raw_ref[b]
        last = raw_ref[jnp.maximum(b - 1, 0)][:, BK - FT :]
        last = jnp.where(b > 0, last, jnp.zeros_like(last))
        before = jnp.concatenate([last, now[:, : BK - FT]], axis=1)
        return jnp.concatenate([before, now, ones], axis=0)

    def norm(x, gram):
        y = gram[:ROWS] + gram[ROWS:]
        return lax.rsqrt(jnp.sum(x.astype(F32) * y, axis=0, keepdims=True) + EPS)

    def scaled(x, r):
        tail = jnp.where(row == 0, r, jnp.where(row == 1, 1.0, 0.0))
        return jnp.concatenate([x[:128].astype(F32) * r, tail], axis=0).astype(BF16).T

    def prepare(b):
        inside = jnp.minimum(b, NB - 1)
        x = features(inside)
        big = dot(mg_ref[...], x)
        r = norm(x, big[HEADS * HD :])
        cos = jnp.concatenate([ct_ref[inside], cs_ref[...]], axis=0) * r
        sin = jnp.concatenate([st_ref[inside], ss_ref[...]], axis=0) * r
        cos, sin = cos.astype(BF16), sin.astype(BF16)
        end = jnp.where(row == 0, end_early, end_late)
        mask = jnp.where((row < 2) & (b * BF + lane_frame >= end), FAR, 0.0).astype(BF16)

        def keys(h):
            first, second = big[h * HD : h * HD + 64], big[h * HD + 64 : h * HD + HD]
            first, second = first.astype(BF16), second.astype(BF16)
            return jnp.concatenate(
                [
                    (first * cos - second * sin).astype(BF16),
                    (first * sin + second * cos).astype(BF16),
                    mask,
                ],
                axis=0,
            )

        return keys, lambda: scaled(x, r)

    for i in range(2):
        frame = own_frames[i]
        rows = pl.ds(pl.multiple_of((frame % BF) * FT, FT), FT)
        x = features(frame // BF)
        own_ref[...] = x.T
        res_ref[4, pl.ds(i * FT, FT), :] = dot(own_ref[rows, :], pw_ref[...]).astype(BF16)
        own_ref[...] = scaled(x, norm(x, dot(mg_ref[HEADS * HD :], x)))
        own = own_ref[rows, :]
        lane = lax.broadcasted_iota(jnp.int32, (FT, ROWS - 128), 1)
        select = (lane == i).astype(F32).astype(BF16)
        cos = cq_ref[...] + tq_ref[0, pl.ds(frame, 1), :]
        sin = sq_ref[...] + tq_ref[1, pl.ds(frame, 1), :]
        for h in range(HEADS):
            pre = dot(own, mq_ref[:, pl.ds(h * HD, HD)])
            rotated = pre * cos + pltpu.roll(pre, 64, 1) * sin
            q_ref[i, h] = jnp.concatenate([rotated.astype(BF16), select], axis=1)

    tokens_copy = pltpu.make_async_copy(res_ref.at[4], tokens_ref, out_sems.at[4])
    tokens_copy.start()
    u_ref[...] = jnp.zeros_like(u_ref)

    def fill(b):
        keys, values = prepare(b)
        for h in range(HEADS):
            k_ref[h] = keys(h)
        v_ref[...] = values()

    def visit(frames, b, carry):
        keys, values = prepare(b + 1)
        for h in range(HEADS):
            q = jnp.concatenate([q_ref[i, h] for i in frames], axis=0)
            w = jnp.exp2(dot(q, k_ref[h])).astype(BF16)
            k_ref[h] = keys(h)
            for n, i in enumerate(frames):
                w_ref[i, pl.ds(h * FT, FT)] = w[n * FT : (n + 1) * FT]
        for i in frames:
            u_ref[i] += dot(w_ref[i], v_ref[...])
        v_ref[...] = values()
        return carry

    fill(0)
    lax.fori_loop(0, blocks_early, functools.partial(visit, (0, 1)), 0)
    lax.fori_loop(blocks_early, blocks_late, functools.partial(visit, (1,)), 0)

    def finish():
        good = jnp.ones((FT, 1), F32)
        for i in range(2):
            for h in range(HEADS):
                u = u_ref[i, pl.ds(h * FT, FT)]
                total = u[:, 129:130]
                good = jnp.where((total >= LOW) & (total <= HIGH), good, 0.0)
                mixed = (u / total).astype(BF16)
                ho_ref[pl.ds(i * FT, FT), pl.ds(h * HD, HD)] = dot(
                    mixed, mv_ref[:, pl.ds(h * HD, HD)]
                ).astype(BF16)
        return jnp.min(good) > 0.5

    bad = jnp.logical_not(finish())

    @pl.when(bad)
    def _():
        u_ref[...] = jnp.zeros_like(u_ref)
        m_ref[...] = jnp.full_like(m_ref, FAR)

        def visit_again(b, carry):
            fill(b)
            for h in range(HEADS):
                k = k_ref[h]
                rows = pl.ds(h * FT, FT)
                for i in range(2):
                    s = dot(q_ref[i, h], k)
                    old = m_ref[i, rows]
                    new = jnp.maximum(old, jnp.max(s, axis=1, keepdims=True))
                    w = jnp.exp2(s - new).astype(BF16)
                    u_ref[i, rows] = u_ref[i, rows] * jnp.exp2(old - new) + dot(w, v_ref[...])
                    m_ref[i, rows] = new
            return carry

        lax.fori_loop(0, blocks_late, visit_again, 0)
        finish()

    sent = [tokens_copy]
    wide_copy.wait()
    for n in (3, 2, 1, 0):
        group = (chip ^ (n // 2)) * 2 + (core ^ (n % 2))
        columns = pl.ds(pl.multiple_of(group * 768, 768), 768)
        res_ref[n] = dot(ho_ref[...], wide_ref[:, columns]).astype(BF16)
        sent.append(pltpu.make_async_copy(res_ref.at[n], outs[n], out_sems.at[n]))
        sent[-1].start()
    for copy in sent:
        copy.wait()


def attention(*arrays):
    vmem = pl.BlockSpec(memory_space=pltpu.VMEM)
    hbm = pl.BlockSpec(memory_space=pl.ANY)
    shape = jax.ShapeDtypeStruct((2 * FT, 768), BF16)
    return pl.pallas_call(
        kernel,
        in_specs=[pl.BlockSpec(memory_space=pltpu.SMEM)] * 3 + [hbm] * 8 + [vmem] * 11 + [hbm],
        out_specs=(hbm,) * 5,
        out_shape=(shape,) * 5,
        scratch_shapes=[
            pltpu.VMEM((NB, 64, BK), BF16),
            pltpu.VMEM((BK, ROWS), BF16),
            pltpu.VMEM((2, HEADS, FT, ROWS), BF16),
            pltpu.VMEM((2, HEADS * FT, BK), BF16),
            pltpu.VMEM((2, HEADS * FT, ROWS), F32),
            pltpu.VMEM((2 * FT, HEADS * HD), BF16),
            pltpu.VMEM((2, HEADS * FT, 1), F32),
            pltpu.VMEM((HEADS, ROWS, BK), BF16),
            pltpu.VMEM((BK, ROWS), BF16),
            pltpu.VMEM((5, 2 * FT, HEADS * HD), BF16),
            pltpu.VMEM((HEADS * HD, 4 * HEADS * HD), BF16),
            pltpu.SemaphoreType.DMA((32,)),
            pltpu.SemaphoreType.DMA((5,)),
            pltpu.SemaphoreType.DMA,
        ],
        compiler_params=pltpu.CompilerParams(vmem_limit_bytes=52 * 2**20),
    )(*arrays)


def permute(x, axis, to):
    return lax.ppermute(x, axis, [(i, to(i)) for i in range(lax.axis_size(axis))])


def weights_kernel(me, p0, p1, p2, p3, gain, wq, wk, wv, mg_ref, mq_ref, mv_ref, aq, ak, av, ag):
    k = pl.program_id(0)

    @pl.when(k == 0)
    def _():
        for ref in (aq, ak, av, ag):
            ref[...] = jnp.zeros_like(ref)

    part = jnp.where(k < 2, jnp.where(k == 0, p0[...], p1[...]), jnp.where(k == 2, p2[...], p3[...]))
    wide = part.astype(F32)
    bias = wide[128:129] + wide[129:130] + wide[130:131]
    row = lax.broadcasted_iota(jnp.int32, (ROWS - 128, part.shape[1]), 0)
    gained = jnp.concatenate([wide[:128], jnp.where(row == 0, bias, 0.0)], axis=0) * gain[0]
    gained = gained.astype(BF16)
    aq[...] += dot(gained, wq[...])
    ak[...] += dot(gained, wk[...])
    av[...] += dot(gained, wv[...])
    ag[...] += lax.dot_general(part, part, (((1,), (1,)), ((), ())), preferred_element_type=F32)

    @pl.when(k == 3)
    def _():
        mq_ref[...] = aq[...].astype(BF16)
        mv_ref[...] = av[...].astype(BF16)
        mg_ref[: HEADS * HD, :] = ak[...].T.astype(BF16)
        gram = ag[...] * (1.0 / (4 * part.shape[1]))
        high = gram.astype(BF16)
        mg_ref[HEADS * HD : HEADS * HD + ROWS, :] = high
        mg_ref[HEADS * HD + ROWS :, :] = (gram - high.astype(F32)).astype(BF16)


def through(parts, gain, wq, wk, wv):
    columns = HEADS * HD
    whole = lambda *shape: pl.BlockSpec(shape, lambda k, me: (0,) * len(shape))
    source = lambda k, me: me[0] ^ k
    weight = pl.BlockSpec((columns, columns), lambda k, me: (source(k, me), 0))
    return pl.pallas_call(
        weights_kernel,
        grid_spec=pltpu.PrefetchScalarGridSpec(
            num_scalar_prefetch=1,
            grid=(4,),
            in_specs=[whole(ROWS, columns)] * 4
            + [pl.BlockSpec((1, 1, columns), lambda k, me: (source(k, me), 0, 0))]
            + [weight] * 3,
            out_specs=[
                whole(columns + 2 * ROWS, ROWS),
                whole(ROWS, columns),
                whole(ROWS, columns),
            ],
            scratch_shapes=[pltpu.VMEM((ROWS, columns), F32)] * 3 + [pltpu.VMEM((ROWS, ROWS), F32)],
        ),
        out_shape=[
            jax.ShapeDtypeStruct((columns + 2 * ROWS, ROWS), BF16),
            jax.ShapeDtypeStruct((ROWS, columns), BF16),
            jax.ShapeDtypeStruct((ROWS, columns), BF16),
        ],
        compiler_params=pltpu.CompilerParams(vmem_limit_bytes=57 * 2**20),
        cost_estimate=pl.CostEstimate(
            flops=2 * ROWS * 3072 * 2400, bytes_accessed=3 * 3072 * 768 * 2, transcendentals=0
        ),
    )(lax.axis_index("head").astype(jnp.int32).reshape(1), *parts, gain.reshape(4, 1, columns), wq, wk, wv)


def widen_kernel(weight, bias, out):
    out[:128] = weight[...]
    b = bias[...]
    row = lax.broadcasted_iota(jnp.int32, (ROWS - 128, b.shape[1]), 0)
    b0 = b.astype(BF16).astype(F32)
    b1 = (b - b0).astype(BF16).astype(F32)
    b2 = b - b0 - b1
    parts = jnp.where(row == 0, b0, jnp.where(row == 1, b1, jnp.where(row == 2, b2, 0.0)))
    out[128:] = parts.astype(BF16)


def widen(weight, bias):
    vmem = pl.BlockSpec(memory_space=pltpu.VMEM)
    return pl.pallas_call(
        widen_kernel,
        in_specs=[vmem] * 2,
        out_specs=vmem,
        out_shape=jax.ShapeDtypeStruct((ROWS, weight.shape[1]), BF16),
        compiler_params=pltpu.CompilerParams(vmem_limit_bytes=2 * 2**20),
        cost_estimate=pl.CostEstimate(flops=0, bytes_accessed=400000, transcendentals=0),
    )(weight, bias.reshape(1, -1))


def join_kernel(z, p0, p1, p2, p3, out):
    for place in range(4):
        k = (z[0] + 4 - place) % 4
        part = jnp.where(k < 2, jnp.where(k == 0, p0[...], p1[...]), jnp.where(k == 2, p2[...], p3[...]))
        out[0, :, place * FT : (place + 1) * FT] = part[:, :FT]
        out[1, :, (3 - place) * FT : (4 - place) * FT] = part[:, FT:]


def join(z, parts):
    vmem = pl.BlockSpec(memory_space=pltpu.VMEM)
    return pl.pallas_call(
        join_kernel,
        in_specs=[pl.BlockSpec(memory_space=pltpu.SMEM)] + [vmem] * 4,
        out_specs=vmem,
        out_shape=jax.ShapeDtypeStruct((2, 32, BK), BF16),
        compiler_params=pltpu.CompilerParams(vmem_limit_bytes=2 * 2**20),
        cost_estimate=pl.CostEstimate(flops=0, bytes_accessed=200000, transcendentals=0),
    )(z.astype(jnp.int32).reshape(1), *parts)


def all_latents(half):
    seq = lax.axis_index("seq")

    def place(i):
        return i // 8, (i // 4) % 2, i % 4

    def at(x, y, z):
        return (x * 2 + y) * 4 + z

    def to_y(i):
        x, y, z = place(i)
        return at(x, 1 - y, z)

    def to_z(k, i):
        x, y, z = place(i)
        return at(x, y, (z + k) % 4)

    def to_x(k, i):
        x, y, z = place(i)
        return at((x + k) % 4, y, z)

    parts = [half] + [permute(half, "seq", functools.partial(to_z, k)) for k in (1, 2, 3)]
    block = join(seq % 4, parts)
    pair = jnp.stack([block, permute(block, "seq", to_y)])
    return [pair] + [permute(pair, "seq", functools.partial(to_x, k)) for k in (1, 2, 3)]


def swap(x, bit):
    return permute(x, "head", lambda i: i ^ bit)


def add(a, b):
    return a.astype(F32) + b.astype(F32)


def local(
    latents,
    span_ids,
    patch_weight,
    patch_bias,
    norm_gain,
    query_weight,
    key_weight,
    value_weight,
    out_weight,
):
    seq = lax.axis_index("seq")
    head = lax.axis_index("head")
    half = lax.dynamic_slice_in_dim(latents, (head % 2) * 32, 32, 0)
    halves = all_latents(half)

    wide = widen(lax.optimization_barrier((patch_weight, half))[0], patch_bias)
    far_part = swap(wide, 2)
    parts = [wide, swap(wide, 1), far_part, swap(far_part, 1)]
    mg, mq, mv = through(parts, norm_gain, query_weight, key_weight, value_weight)
    others = [swap(halves[0], 1)] + [
        swap(lax.optimization_barrier((part, mq))[0], 1) for part in halves[1:]
    ]
    pieces = [piece for pair in zip(halves, others) for piece in pair]

    w_t, _, _ = frequencies()
    spatial = spatial_angles()
    cs = jnp.asarray(np.tile(np.cos(spatial).T, (1, BF)), F32)
    ss = jnp.asarray(np.tile(np.sin(spatial).T, (1, BF)), F32)
    temporal = np.outer(np.arange(FRAMES), w_t)
    by_block = np.repeat(temporal.reshape(NB, BF, 16).transpose(0, 2, 1), FT, axis=2)
    ct = jnp.asarray(np.cos(by_block), F32)
    st = jnp.asarray(np.sin(by_block), F32)
    nothing = np.zeros((FT, 16))
    cq = np.concatenate([nothing, np.cos(spatial)], axis=1)
    sq = np.concatenate([nothing, np.sin(spatial)], axis=1)
    rest = np.zeros((FRAMES, 48))
    tc = np.concatenate([np.cos(temporal), rest], axis=1)
    ts = np.concatenate([np.sin(temporal), rest], axis=1)
    cq = jnp.asarray(np.concatenate([cq, cq], axis=1) * SCALE, F32)
    sq = jnp.asarray(np.concatenate([-sq, sq], axis=1) * SCALE, F32)
    tq = np.stack([np.concatenate([tc, tc], axis=1), np.concatenate([-ts, ts], axis=1)])
    tq = jnp.asarray(tq * SCALE, F32)

    near, near_other, far, far_other, tokens = attention(
        seq.astype(jnp.int32).reshape(1),
        head.astype(jnp.int32).reshape(1),
        span_ids,
        *pieces,
        *(mg, mq, mv, wide, cs, ss, ct, st, cq, sq, tq, out_weight),
    )
    sent = swap(add(far, swap(far_other, 1)).astype(BF16), 2)
    kept = add(near, swap(near_other, 1)).astype(BF16)
    return (add(kept, sent) + tokens.astype(F32)).astype(BF16)


def solution(mesh):
    return jax.shard_map(
        local,
        mesh=mesh,
        in_specs=(
            P(None, "seq"),
            P(),
            P(None, "head"),
            P("head"),
            P(),
            P(None, "head"),
            P(None, "head"),
            P(None, "head"),
            P("head", None),
        ),
        out_specs=P("seq", "head"),
        check_vma=False,
    )
```

```python
import functools
import math

import jax
import jax.numpy as jnp
import numpy as np
from jax import lax
from jax.experimental import pallas as pl
from jax.experimental.pallas import tpu as pltpu
from jax.sharding import PartitionSpec as P

HD = 128
HEADS = 6
FT = 192
FRAMES = 64
BF = 4
BK = BF * FT
NB = FRAMES // BF
ROWS = 144
WIDTH = 24
EPS = 1e-06
YARN = 4.0
SCALE = (0.1 * math.log(YARN) + 1.0) ** 2 / math.sqrt(HD) * math.log2(math.e)
FAR = -1e30
LOW, HIGH = 2.0**-60, 2.0**100

F32 = jnp.float32
BF16 = jnp.bfloat16


def spectrum(count):
    return np.exp(-math.log(10000.0) * np.arange(count) / count)


def frequencies():
    pairs = HD // 2
    count_t, count_h = pairs // 4, 3 * pairs // 8
    base_t = spectrum(count_t)
    ramp = np.clip((FRAMES / 4.0 / (2.0 * math.pi / base_t) - 1.0) / 31.0, 0.0, 1.0)
    return base_t * (ramp + (1.0 - ramp) / YARN), spectrum(count_h), spectrum(pairs - count_t - count_h)


def spatial_angles():
    _, w_h, w_w = frequencies()
    inner = np.arange(FT)
    return np.concatenate(
        [np.outer(inner // WIDTH, w_h), np.outer(inner % WIDTH, w_w)], axis=1
    )


def dot(a, b):
    return jnp.dot(a, b, preferred_element_type=F32)


def kernel(seq_ref, head_ref, span_ref, *refs):
    pieces, refs = refs[:8], refs[8:]
    (mg_ref, mq_ref, mv_ref, pw_ref, cs_ref, ss_ref, ct_ref, st_ref, cq_ref, sq_ref, tq_ref, wo_ref) = refs[:12]
    (outs, tokens_ref), refs = (refs[12:16], refs[16]), refs[17:]
    raw_ref, own_ref, q_ref, w_ref, u_ref, ho_ref, m_ref, k_ref, v_ref, res_ref, wide_ref, sems, out_sems, wide_sem = refs
    seq, head = seq_ref[0], head_ref[0]
    own_frames = (seq, FRAMES - 1 - seq)

    wide_copy = pltpu.make_async_copy(wo_ref, wide_ref, wide_sem)
    wide_copy.start()
    x_at, y_at, core, chip = seq // 8, (seq // 4) % 2, head % 2, head // 2

    copies = []
    for k in range(4):
        for c in range(2):
            rows = pl.ds(pl.multiple_of((core ^ c) * 32, 32), 32)
            for i in range(2):
                group = ((x_at + 4 - k) % 4) * 2 + (y_at ^ i)
                for late in range(2):
                    block = NB - 1 - group if late else group
                    copies.append(
                        pltpu.make_async_copy(
                            pieces[2 * k + c].at[i, late],
                            raw_ref.at[block, rows],
                            sems.at[len(copies)],
                        )
                    )
    for copy in copies:
        copy.start()

    def end_of(frame):
        count = lambda g, seen: seen + (span_ref[g] <= span_ref[frame]).astype(jnp.int32)
        return lax.fori_loop(0, FRAMES, count, 0, unroll=True)

    end_early, end_late = end_of(own_frames[0]), end_of(own_frames[1])
    blocks_early = (end_early + BF - 1) // BF
    blocks_late = (end_late + BF - 1) // BF
    for copy in copies:
        copy.wait()

    row = lax.broadcasted_iota(jnp.int32, (ROWS - 128, BK), 0)
    lane_frame = lax.broadcasted_iota(jnp.int32, (ROWS - 128, BK), 1) // FT
    ones = (row < 3).astype(F32).astype(BF16)

    def features(b):
        now = raw_ref[b]
        last = raw_ref[jnp.maximum(b - 1, 0)][:, BK - FT :]
        last = jnp.where(b > 0, last, jnp.zeros_like(last))
        before = jnp.concatenate([last, now[:, : BK - FT]], axis=1)
        return jnp.concatenate([before, now, ones], axis=0)

    def norm(x, gram):
        y = gram[:ROWS] + gram[ROWS:]
        return lax.rsqrt(jnp.sum(x.astype(F32) * y, axis=0, keepdims=True) + EPS)

    def scaled(x, r):
        tail = jnp.where(row == 0, r, jnp.where(row == 1, 1.0, 0.0))
        return jnp.concatenate([x[:128].astype(F32) * r, tail], axis=0).astype(BF16).T

    def prepare(b):
        inside = jnp.minimum(b, NB - 1)
        x = features(inside)
        big = dot(mg_ref[...], x)
        r = norm(x, big[HEADS * HD :])
        cos = jnp.concatenate([ct_ref[inside], cs_ref[...]], axis=0) * r
        sin = jnp.concatenate([st_ref[inside], ss_ref[...]], axis=0) * r
        cos, sin = cos.astype(BF16), sin.astype(BF16)
        end = jnp.where(row == 0, end_early, end_late)
        mask = jnp.where((row < 2) & (b * BF + lane_frame >= end), FAR, 0.0).astype(BF16)

        def keys(h):
            first, second = big[h * HD : h * HD + 64], big[h * HD + 64 : h * HD + HD]
            first, second = first.astype(BF16), second.astype(BF16)
            return jnp.concatenate(
                [
                    (first * cos - second * sin).astype(BF16),
                    (first * sin + second * cos).astype(BF16),
                    mask,
                ],
                axis=0,
            )

        return keys, lambda: scaled(x, r)

    for i in range(2):
        frame = own_frames[i]
        rows = pl.ds(pl.multiple_of((frame % BF) * FT, FT), FT)
        x = features(frame // BF)
        own_ref[...] = x.T
        res_ref[4, pl.ds(i * FT, FT), :] = dot(own_ref[rows, :], pw_ref[...]).astype(BF16)
        own_ref[...] = scaled(x, norm(x, dot(mg_ref[HEADS * HD :], x)))
        own = own_ref[rows, :]
        lane = lax.broadcasted_iota(jnp.int32, (FT, ROWS - 128), 1)
        select = (lane == i).astype(F32).astype(BF16)
        cos = cq_ref[...] + tq_ref[0, pl.ds(frame, 1), :]
        sin = sq_ref[...] + tq_ref[1, pl.ds(frame, 1), :]
        for h in range(HEADS):
            pre = dot(own, mq_ref[:, pl.ds(h * HD, HD)])
            rotated = pre * cos + pltpu.roll(pre, 64, 1) * sin
            q_ref[i, h] = jnp.concatenate([rotated.astype(BF16), select], axis=1)

    tokens_copy = pltpu.make_async_copy(res_ref.at[4], tokens_ref, out_sems.at[4])
    tokens_copy.start()
    u_ref[...] = jnp.zeros_like(u_ref)

    def fill(b):
        keys, values = prepare(b)
        for h in range(HEADS):
            k_ref[h] = keys(h)
        v_ref[...] = values()

    def visit(frames, b, carry):
        keys, values = prepare(b + 1)
        for h in range(HEADS):
            q = jnp.concatenate([q_ref[i, h] for i in frames], axis=0)
            w = jnp.exp2(dot(q, k_ref[h])).astype(BF16)
            k_ref[h] = keys(h)
            for n, i in enumerate(frames):
                w_ref[i, pl.ds(h * FT, FT)] = w[n * FT : (n + 1) * FT]
        for i in frames:
            u_ref[i] += dot(w_ref[i], v_ref[...])
        v_ref[...] = values()
        return carry

    fill(0)
    lax.fori_loop(0, blocks_early, functools.partial(visit, (0, 1)), 0)
    lax.fori_loop(blocks_early, blocks_late, functools.partial(visit, (1,)), 0)

    def finish():
        good = jnp.ones((FT, 1), F32)
        for i in range(2):
            for h in range(HEADS):
                u = u_ref[i, pl.ds(h * FT, FT)]
                total = u[:, 129:130]
                good = jnp.where((total >= LOW) & (total <= HIGH), good, 0.0)
                mixed = (u / total).astype(BF16)
                ho_ref[pl.ds(i * FT, FT), pl.ds(h * HD, HD)] = dot(
                    mixed, mv_ref[:, pl.ds(h * HD, HD)]
                ).astype(BF16)
        return jnp.min(good) > 0.5

    bad = jnp.logical_not(finish())

    @pl.when(bad)
    def _():
        u_ref[...] = jnp.zeros_like(u_ref)
        m_ref[...] = jnp.full_like(m_ref, FAR)

        def visit_again(b, carry):
            fill(b)
            for h in range(HEADS):
                k = k_ref[h]
                rows = pl.ds(h * FT, FT)
                for i in range(2):
                    s = dot(q_ref[i, h], k)
                    old = m_ref[i, rows]
                    new = jnp.maximum(old, jnp.max(s, axis=1, keepdims=True))
                    w = jnp.exp2(s - new).astype(BF16)
                    u_ref[i, rows] = u_ref[i, rows] * jnp.exp2(old - new) + dot(w, v_ref[...])
                    m_ref[i, rows] = new
            return carry

        lax.fori_loop(0, blocks_late, visit_again, 0)
        finish()

    sent = [tokens_copy]
    wide_copy.wait()
    for n in (3, 2, 1, 0):
        group = (chip ^ (n // 2)) * 2 + (core ^ (n % 2))
        columns = pl.ds(pl.multiple_of(group * 768, 768), 768)
        res_ref[n] = dot(ho_ref[...], wide_ref[:, columns]).astype(BF16)
        sent.append(pltpu.make_async_copy(res_ref.at[n], outs[n], out_sems.at[n]))
        sent[-1].start()
    for copy in sent:
        copy.wait()


def attention(*arrays):
    vmem = pl.BlockSpec(memory_space=pltpu.VMEM)
    hbm = pl.BlockSpec(memory_space=pl.ANY)
    shape = jax.ShapeDtypeStruct((2 * FT, 768), BF16)
    return pl.pallas_call(
        kernel,
        in_specs=[pl.BlockSpec(memory_space=pltpu.SMEM)] * 3 + [hbm] * 8 + [vmem] * 11 + [hbm],
        out_specs=(hbm,) * 5,
        out_shape=(shape,) * 5,
        scratch_shapes=[
            pltpu.VMEM((NB, 64, BK), BF16),
            pltpu.VMEM((BK, ROWS), BF16),
            pltpu.VMEM((2, HEADS, FT, ROWS), BF16),
            pltpu.VMEM((2, HEADS * FT, BK), BF16),
            pltpu.VMEM((2, HEADS * FT, ROWS), F32),
            pltpu.VMEM((2 * FT, HEADS * HD), BF16),
            pltpu.VMEM((2, HEADS * FT, 1), F32),
            pltpu.VMEM((HEADS, ROWS, BK), BF16),
            pltpu.VMEM((BK, ROWS), BF16),
            pltpu.VMEM((5, 2 * FT, HEADS * HD), BF16),
            pltpu.VMEM((HEADS * HD, 4 * HEADS * HD), BF16),
            pltpu.SemaphoreType.DMA((32,)),
            pltpu.SemaphoreType.DMA((5,)),
            pltpu.SemaphoreType.DMA,
        ],
        compiler_params=pltpu.CompilerParams(vmem_limit_bytes=52 * 2**20),
    )(*arrays)


def permute(x, axis, to):
    return lax.ppermute(x, axis, [(i, to(i)) for i in range(lax.axis_size(axis))])


def weights_kernel(first, me, p0, p1, gain, wq, wk, wv, *refs):
    k = pl.program_id(0)
    sums = refs[:4] if first else refs[7:]

    @pl.when(k == 0)
    def _():
        for n, ref in enumerate(sums):
            ref[...] = jnp.zeros_like(ref) if first else refs[n][...]

    aq, ak, av, ag = sums
    part = jnp.where(k == 0, p0[...], p1[...])
    wide = part.astype(F32)
    bias = wide[128:129] + wide[129:130] + wide[130:131]
    row = lax.broadcasted_iota(jnp.int32, (ROWS - 128, part.shape[1]), 0)
    gained = jnp.concatenate([wide[:128], jnp.where(row == 0, bias, 0.0)], axis=0) * gain[0]
    gained = gained.astype(BF16)
    aq[...] += dot(gained, wq[...])
    ak[...] += dot(gained, wk[...])
    av[...] += dot(gained, wv[...])
    ag[...] += lax.dot_general(part, part, (((1,), (1,)), ((), ())), preferred_element_type=F32)
    if first:
        return
    mg_ref, mq_ref, mv_ref = refs[4:7]

    @pl.when(k == 1)
    def _():
        mq_ref[...] = aq[...].astype(BF16)
        mv_ref[...] = av[...].astype(BF16)
        mg_ref[: HEADS * HD, :] = ak[...].T.astype(BF16)
        gram = ag[...] * (1.0 / (4 * part.shape[1]))
        high = gram.astype(BF16)
        mg_ref[HEADS * HD : HEADS * HD + ROWS, :] = high
        mg_ref[HEADS * HD + ROWS :, :] = (gram - high.astype(F32)).astype(BF16)


def through(parts, gain, wq, wk, wv, sums=()):
    columns, first = HEADS * HD, not sums
    whole = lambda *shape: pl.BlockSpec(shape, lambda k, me: (0,) * len(shape))
    source = lambda k, me: me[0] ^ (k if first else k + 2)
    weight = pl.BlockSpec((columns, columns), lambda k, me: (source(k, me), 0))
    sizes = [(ROWS, columns)] * 3 + [(ROWS, ROWS)]
    results = sizes if first else [(columns + 2 * ROWS, ROWS), (ROWS, columns), (ROWS, columns)]
    return pl.pallas_call(
        functools.partial(weights_kernel, first),
        grid_spec=pltpu.PrefetchScalarGridSpec(
            num_scalar_prefetch=1,
            grid=(2,),
            in_specs=[whole(ROWS, columns)] * 2
            + [pl.BlockSpec((1, 1, columns), lambda k, me: (source(k, me), 0, 0))]
            + [weight] * 3
            + ([] if first else [whole(*size) for size in sizes]),
            out_specs=[whole(*size) for size in results],
            scratch_shapes=[] if first else [pltpu.VMEM(size, F32) for size in sizes],
        ),
        out_shape=[jax.ShapeDtypeStruct(size, F32 if first else BF16) for size in results],
        compiler_params=pltpu.CompilerParams(vmem_limit_bytes=57 * 2**20),
        cost_estimate=pl.CostEstimate(
            flops=ROWS * 3072 * 2400, bytes_accessed=3 * 1536 * 768 * 2, transcendentals=0
        ),
    )(
        lax.axis_index("head").astype(jnp.int32).reshape(1),
        *parts,
        gain.reshape(4, 1, columns),
        *(wq, wk, wv, *sums),
    )


def join_kernel(z, p0, p1, p2, p3, out):
    for place in range(4):
        k = (z[0] + 4 - place) % 4
        part = jnp.where(k < 2, jnp.where(k == 0, p0[...], p1[...]), jnp.where(k == 2, p2[...], p3[...]))
        out[0, :, place * FT : (place + 1) * FT] = part[:, :FT]
        out[1, :, (3 - place) * FT : (4 - place) * FT] = part[:, FT:]


def join(z, parts):
    vmem = pl.BlockSpec(memory_space=pltpu.VMEM)
    return pl.pallas_call(
        join_kernel,
        in_specs=[pl.BlockSpec(memory_space=pltpu.SMEM)] + [vmem] * 4,
        out_specs=vmem,
        out_shape=jax.ShapeDtypeStruct((2, 32, BK), BF16),
        compiler_params=pltpu.CompilerParams(vmem_limit_bytes=2 * 2**20),
        cost_estimate=pl.CostEstimate(flops=0, bytes_accessed=200000, transcendentals=0),
    )(z.astype(jnp.int32).reshape(1), *parts)


def all_latents(half, beside):
    seq = lax.axis_index("seq")

    def place(i):
        return i // 8, (i // 4) % 2, i % 4

    def at(x, y, z):
        return (x * 2 + y) * 4 + z

    def to_y(i):
        x, y, z = place(i)
        return at(x, 1 - y, z)

    def to_z(k, i):
        x, y, z = place(i)
        return at(x, y, (z + k) % 4)

    def to_x(k, i):
        x, y, z = place(i)
        return at((x + k) % 4, y, z)

    parts = [half] + [permute(half, "seq", functools.partial(to_z, k)) for k in (1, 2, 3)]
    block = join(seq % 4, parts)
    received = lax.optimization_barrier((permute(block, "seq", to_y), *beside))[0]
    pair = jnp.stack([block, received])
    return [pair] + [permute(pair, "seq", functools.partial(to_x, k)) for k in (1, 2, 3)]


def swap(x, bit):
    return permute(x, "head", lambda i: i ^ bit)


def add(a, b):
    return a.astype(F32) + b.astype(F32)


def local(
    latents,
    span_ids,
    patch_weight,
    patch_bias,
    norm_gain,
    query_weight,
    key_weight,
    value_weight,
    out_weight,
):
    seq = lax.axis_index("seq")
    head = lax.axis_index("head")
    half = lax.dynamic_slice_in_dim(latents, (head % 2) * 32, 32, 0)

    b0 = patch_bias.astype(BF16)
    b1 = (patch_bias - b0.astype(F32)).astype(BF16)
    b2 = (patch_bias - b0.astype(F32) - b1.astype(F32)).astype(BF16)
    rest = jnp.zeros((ROWS - 131, patch_bias.shape[0]), BF16)
    wide = jnp.concatenate([patch_weight, b0[None], b1[None], b2[None], rest], axis=0)
    far_part = swap(wide, 2)
    projections = norm_gain, query_weight, key_weight, value_weight
    sums = through([wide, swap(wide, 1)], *projections)
    halves = all_latents(half, sums)
    mg, mq, mv = through([far_part, swap(far_part, 1)], *projections, tuple(sums))
    others = [swap(halves[0], 1)] + [
        swap(lax.optimization_barrier((part, mq))[0], 1) for part in halves[1:]
    ]
    pieces = [piece for pair in zip(halves, others) for piece in pair]

    w_t, _, _ = frequencies()
    spatial = spatial_angles()
    cs = jnp.asarray(np.tile(np.cos(spatial).T, (1, BF)), F32)
    ss = jnp.asarray(np.tile(np.sin(spatial).T, (1, BF)), F32)
    temporal = np.outer(np.arange(FRAMES), w_t)
    by_block = np.repeat(temporal.reshape(NB, BF, 16).transpose(0, 2, 1), FT, axis=2)
    ct = jnp.asarray(np.cos(by_block), F32)
    st = jnp.asarray(np.sin(by_block), F32)
    nothing = np.zeros((FT, 16))
    cq = np.concatenate([nothing, np.cos(spatial)], axis=1)
    sq = np.concatenate([nothing, np.sin(spatial)], axis=1)
    rest = np.zeros((FRAMES, 48))
    tc = np.concatenate([np.cos(temporal), rest], axis=1)
    ts = np.concatenate([np.sin(temporal), rest], axis=1)
    cq = jnp.asarray(np.concatenate([cq, cq], axis=1) * SCALE, F32)
    sq = jnp.asarray(np.concatenate([-sq, sq], axis=1) * SCALE, F32)
    tq = np.stack([np.concatenate([tc, tc], axis=1), np.concatenate([-ts, ts], axis=1)])
    tq = jnp.asarray(tq * SCALE, F32)

    near, near_other, far, far_other, tokens = attention(
        seq.astype(jnp.int32).reshape(1),
        head.astype(jnp.int32).reshape(1),
        span_ids,
        *pieces,
        *(mg, mq, mv, wide, cs, ss, ct, st, cq, sq, tq, out_weight),
    )
    sent = swap(add(far, swap(far_other, 1)).astype(BF16), 2)
    kept = add(near, swap(near_other, 1)).astype(BF16)
    return (add(kept, sent) + tokens.astype(F32)).astype(BF16)


def solution(mesh):
    return jax.shard_map(
        local,
        mesh=mesh,
        in_specs=(
            P(None, "seq"),
            P(),
            P(None, "head"),
            P("head"),
            P(),
            P(None, "head"),
            P(None, "head"),
            P(None, "head"),
            P("head", None),
        ),
        out_specs=P("seq", "head"),
        check_vma=False,
    )
```

```python
import functools
import math

import jax
import jax.numpy as jnp
import numpy as np
from jax import lax
from jax.experimental import pallas as pl
from jax.experimental.pallas import tpu as pltpu
from jax.sharding import PartitionSpec as P

HD = 128
HEADS = 6
FT = 192
FRAMES = 64
BF = 4
BK = BF * FT
NB = FRAMES // BF
ROWS = 144
WIDTH = 24
EPS = 1e-06
YARN = 4.0
SCALE = (0.1 * math.log(YARN) + 1.0) ** 2 / math.sqrt(HD) * math.log2(math.e)
FAR = -1e30
LOW, HIGH = 2.0**-60, 2.0**100

F32 = jnp.float32
BF16 = jnp.bfloat16


def spectrum(count):
    return np.exp(-math.log(10000.0) * np.arange(count) / count)


def frequencies():
    pairs = HD // 2
    count_t, count_h = pairs // 4, 3 * pairs // 8
    base_t = spectrum(count_t)
    ramp = np.clip((FRAMES / 4.0 / (2.0 * math.pi / base_t) - 1.0) / 31.0, 0.0, 1.0)
    return base_t * (ramp + (1.0 - ramp) / YARN), spectrum(count_h), spectrum(pairs - count_t - count_h)


def spatial_angles():
    _, w_h, w_w = frequencies()
    inner = np.arange(FT)
    return np.concatenate(
        [np.outer(inner // WIDTH, w_h), np.outer(inner % WIDTH, w_w)], axis=1
    )


def dot(a, b):
    return jnp.dot(a, b, preferred_element_type=F32)


def kernel(seq_ref, head_ref, span_ref, *refs):
    pieces, refs = refs[:8], refs[8:]
    (mg_ref, mq_ref, mv_ref, pw_ref, cs_ref, ss_ref, ct_ref, st_ref, cq_ref, sq_ref, tq_ref, wo_ref) = refs[:12]
    (outs, tokens_ref), refs = (refs[12:18], refs[18]), refs[19:]
    raw_ref, own_ref, q_ref, w_ref, u_ref, ho_ref, m_ref, k_ref, v_ref, res_ref, wide_ref, sems, out_sems, wide_sem = refs
    seq, head = seq_ref[0], head_ref[0]
    own_frames = (seq, FRAMES - 1 - seq)

    wide_copy = pltpu.make_async_copy(wo_ref, wide_ref, wide_sem)
    wide_copy.start()
    x_at, y_at, core, chip = seq // 8, (seq // 4) % 2, head % 2, head // 2

    copies = []
    for k in range(4):
        for c in range(2):
            rows = pl.ds(pl.multiple_of((core ^ c) * 32, 32), 32)
            for i in range(2):
                group = ((x_at + 4 - k) % 4) * 2 + (y_at ^ i)
                for late in range(2):
                    block = NB - 1 - group if late else group
                    copies.append(
                        pltpu.make_async_copy(
                            pieces[2 * k + c].at[i, late],
                            raw_ref.at[block, rows],
                            sems.at[len(copies)],
                        )
                    )
    for copy in copies:
        copy.start()

    def end_of(frame):
        count = lambda g, seen: seen + (span_ref[g] <= span_ref[frame]).astype(jnp.int32)
        return lax.fori_loop(0, FRAMES, count, 0, unroll=True)

    end_early, end_late = end_of(own_frames[0]), end_of(own_frames[1])
    blocks_early = (end_early + BF - 1) // BF
    blocks_late = (end_late + BF - 1) // BF
    for copy in copies:
        copy.wait()

    row = lax.broadcasted_iota(jnp.int32, (ROWS - 128, BK), 0)
    lane_frame = lax.broadcasted_iota(jnp.int32, (ROWS - 128, BK), 1) // FT
    ones = (row < 3).astype(F32).astype(BF16)

    def features(b):
        now = raw_ref[b]
        last = raw_ref[jnp.maximum(b - 1, 0)][:, BK - FT :]
        last = jnp.where(b > 0, last, jnp.zeros_like(last))
        before = jnp.concatenate([last, now[:, : BK - FT]], axis=1)
        return jnp.concatenate([before, now, ones], axis=0)

    def norm(x, gram):
        y = gram[:ROWS] + gram[ROWS:]
        return lax.rsqrt(jnp.sum(x.astype(F32) * y, axis=0, keepdims=True) + EPS)

    def scaled(x, r):
        tail = jnp.where(row == 0, r, jnp.where(row == 1, 1.0, 0.0))
        return jnp.concatenate([x[:128].astype(F32) * r, tail], axis=0).astype(BF16).T

    def prepare(b):
        inside = jnp.minimum(b, NB - 1)
        x = features(inside)
        big = dot(mg_ref[...], x)
        r = norm(x, big[HEADS * HD :])
        cos = jnp.concatenate([ct_ref[inside], cs_ref[...]], axis=0) * r
        sin = jnp.concatenate([st_ref[inside], ss_ref[...]], axis=0) * r
        cos, sin = cos.astype(BF16), sin.astype(BF16)
        end = jnp.where(row == 0, end_early, end_late)
        mask = jnp.where((row < 2) & (b * BF + lane_frame >= end), FAR, 0.0).astype(BF16)

        def keys(h):
            first, second = big[h * HD : h * HD + 64], big[h * HD + 64 : h * HD + HD]
            first, second = first.astype(BF16), second.astype(BF16)
            return jnp.concatenate(
                [
                    (first * cos - second * sin).astype(BF16),
                    (first * sin + second * cos).astype(BF16),
                    mask,
                ],
                axis=0,
            )

        return keys, lambda: scaled(x, r)

    for i in range(2):
        frame = own_frames[i]
        rows = pl.ds(pl.multiple_of((frame % BF) * FT, FT), FT)
        x = features(frame // BF)
        own_ref[...] = x.T
        res_ref[4, pl.ds(i * FT, FT), :] = dot(own_ref[rows, :], pw_ref[...]).astype(BF16)
        own_ref[...] = scaled(x, norm(x, dot(mg_ref[HEADS * HD :], x)))
        own = own_ref[rows, :]
        lane = lax.broadcasted_iota(jnp.int32, (FT, ROWS - 128), 1)
        select = (lane == i).astype(F32).astype(BF16)
        cos = cq_ref[...] + tq_ref[0, pl.ds(frame, 1), :]
        sin = sq_ref[...] + tq_ref[1, pl.ds(frame, 1), :]
        for h in range(HEADS):
            pre = dot(own, mq_ref[:, pl.ds(h * HD, HD)])
            rotated = pre * cos + pltpu.roll(pre, 64, 1) * sin
            q_ref[i, h] = jnp.concatenate([rotated.astype(BF16), select], axis=1)

    tokens_copy = pltpu.make_async_copy(res_ref.at[4], tokens_ref, out_sems.at[6])
    tokens_copy.start()
    u_ref[...] = jnp.zeros_like(u_ref)

    def fill(b):
        keys, values = prepare(b)
        for h in range(HEADS):
            k_ref[h] = keys(h)
        v_ref[...] = values()

    def visit(frames, b, carry):
        keys, values = prepare(b + 1)
        for h in range(HEADS):
            q = jnp.concatenate([q_ref[i, h] for i in frames], axis=0)
            w = jnp.exp2(dot(q, k_ref[h])).astype(BF16)
            k_ref[h] = keys(h)
            for n, i in enumerate(frames):
                w_ref[i, pl.ds(h * FT, FT)] = w[n * FT : (n + 1) * FT]
        for i in frames:
            u_ref[i] += dot(w_ref[i], v_ref[...])
        v_ref[...] = values()
        return carry

    fill(0)
    lax.fori_loop(0, blocks_early, functools.partial(visit, (0, 1)), 0)
    lax.fori_loop(blocks_early, blocks_late, functools.partial(visit, (1,)), 0)

    def finish():
        good = jnp.ones((FT, 1), F32)
        for i in range(2):
            for h in range(HEADS):
                u = u_ref[i, pl.ds(h * FT, FT)]
                total = u[:, 129:130]
                good = jnp.where((total >= LOW) & (total <= HIGH), good, 0.0)
                mixed = (u / total).astype(BF16)
                ho_ref[pl.ds(i * FT, FT), pl.ds(h * HD, HD)] = dot(
                    mixed, mv_ref[:, pl.ds(h * HD, HD)]
                ).astype(BF16)
        return jnp.min(good) > 0.5

    bad = jnp.logical_not(finish())

    @pl.when(bad)
    def _():
        u_ref[...] = jnp.zeros_like(u_ref)
        m_ref[...] = jnp.full_like(m_ref, FAR)

        def visit_again(b, carry):
            fill(b)
            for h in range(HEADS):
                k = k_ref[h]
                rows = pl.ds(h * FT, FT)
                for i in range(2):
                    s = dot(q_ref[i, h], k)
                    old = m_ref[i, rows]
                    new = jnp.maximum(old, jnp.max(s, axis=1, keepdims=True))
                    w = jnp.exp2(s - new).astype(BF16)
                    u_ref[i, rows] = u_ref[i, rows] * jnp.exp2(old - new) + dot(w, v_ref[...])
                    m_ref[i, rows] = new
            return carry

        lax.fori_loop(0, blocks_late, visit_again, 0)
        finish()

    sent = [tokens_copy]
    wide_copy.wait()
    for n in (3, 2, 1, 0):
        group = (chip ^ (n // 2)) * 2 + (core ^ (n % 2))
        columns = pl.ds(pl.multiple_of(group * 768, 768), 768)
        res_ref[n] = dot(ho_ref[...], wide_ref[:, columns]).astype(BF16)
        for i, target in enumerate(outs[2 * n - 2 : 2 * n] if n > 1 else outs[n : n + 1]):
            source = res_ref.at[n, pl.ds(i * FT, FT)] if n > 1 else res_ref.at[n]
            sent.append(pltpu.make_async_copy(source, target, out_sems.at[len(sent) - 1]))
            sent[-1].start()
    for copy in sent:
        copy.wait()


def attention(*arrays):
    vmem = pl.BlockSpec(memory_space=pltpu.VMEM)
    hbm = pl.BlockSpec(memory_space=pl.ANY)
    shape = jax.ShapeDtypeStruct((2 * FT, 768), BF16)
    frame = jax.ShapeDtypeStruct((FT, 768), BF16)
    return pl.pallas_call(
        kernel,
        in_specs=[pl.BlockSpec(memory_space=pltpu.SMEM)] * 3 + [hbm] * 8 + [vmem] * 11 + [hbm],
        out_specs=(hbm,) * 7,
        out_shape=(shape,) * 2 + (frame,) * 4 + (shape,),
        scratch_shapes=[
            pltpu.VMEM((NB, 64, BK), BF16),
            pltpu.VMEM((BK, ROWS), BF16),
            pltpu.VMEM((2, HEADS, FT, ROWS), BF16),
            pltpu.VMEM((2, HEADS * FT, BK), BF16),
            pltpu.VMEM((2, HEADS * FT, ROWS), F32),
            pltpu.VMEM((2 * FT, HEADS * HD), BF16),
            pltpu.VMEM((2, HEADS * FT, 1), F32),
            pltpu.VMEM((HEADS, ROWS, BK), BF16),
            pltpu.VMEM((BK, ROWS), BF16),
            pltpu.VMEM((5, 2 * FT, HEADS * HD), BF16),
            pltpu.VMEM((HEADS * HD, 4 * HEADS * HD), BF16),
            pltpu.SemaphoreType.DMA((32,)),
            pltpu.SemaphoreType.DMA((7,)),
            pltpu.SemaphoreType.DMA,
        ],
        compiler_params=pltpu.CompilerParams(vmem_limit_bytes=52 * 2**20),
    )(*arrays)


def permute(x, axis, to):
    return lax.ppermute(x, axis, [(i, to(i)) for i in range(lax.axis_size(axis))])


def weights_kernel(me, p0, p1, p2, p3, gain, wq, wk, wv, mg_ref, mq_ref, mv_ref, aq, ak, av, ag):
    k = pl.program_id(0)

    @pl.when(k == 0)
    def _():
        for ref in (aq, ak, av, ag):
            ref[...] = jnp.zeros_like(ref)

    part = jnp.where(k < 2, jnp.where(k == 0, p0[...], p1[...]), jnp.where(k == 2, p2[...], p3[...]))
    wide = part.astype(F32)
    bias = wide[128:129] + wide[129:130] + wide[130:131]
    row = lax.broadcasted_iota(jnp.int32, (ROWS - 128, part.shape[1]), 0)
    gained = jnp.concatenate([wide[:128], jnp.where(row == 0, bias, 0.0)], axis=0) * gain[0]
    gained = gained.astype(BF16)
    aq[...] += dot(gained, wq[...])
    ak[...] += dot(gained, wk[...])
    av[...] += dot(gained, wv[...])
    ag[...] += lax.dot_general(part, part, (((1,), (1,)), ((), ())), preferred_element_type=F32)

    @pl.when(k == 3)
    def _():
        mq_ref[...] = aq[...].astype(BF16)
        mv_ref[...] = av[...].astype(BF16)
        mg_ref[: HEADS * HD, :] = ak[...].T.astype(BF16)
        gram = ag[...] * (1.0 / (4 * part.shape[1]))
        high = gram.astype(BF16)
        mg_ref[HEADS * HD : HEADS * HD + ROWS, :] = high
        mg_ref[HEADS * HD + ROWS :, :] = (gram - high.astype(F32)).astype(BF16)


def through(parts, gain, wq, wk, wv):
    columns = HEADS * HD
    whole = lambda *shape: pl.BlockSpec(shape, lambda k, me: (0,) * len(shape))
    source = lambda k, me: me[0] ^ k
    weight = pl.BlockSpec((columns, columns), lambda k, me: (source(k, me), 0))
    return pl.pallas_call(
        weights_kernel,
        grid_spec=pltpu.PrefetchScalarGridSpec(
            num_scalar_prefetch=1,
            grid=(4,),
            in_specs=[whole(ROWS, columns)] * 4
            + [pl.BlockSpec((1, 1, columns), lambda k, me: (source(k, me), 0, 0))]
            + [weight] * 3,
            out_specs=[
                whole(columns + 2 * ROWS, ROWS),
                whole(ROWS, columns),
                whole(ROWS, columns),
            ],
            scratch_shapes=[pltpu.VMEM((ROWS, columns), F32)] * 3 + [pltpu.VMEM((ROWS, ROWS), F32)],
        ),
        out_shape=[
            jax.ShapeDtypeStruct((columns + 2 * ROWS, ROWS), BF16),
            jax.ShapeDtypeStruct((ROWS, columns), BF16),
            jax.ShapeDtypeStruct((ROWS, columns), BF16),
        ],
        compiler_params=pltpu.CompilerParams(vmem_limit_bytes=57 * 2**20),
        cost_estimate=pl.CostEstimate(
            flops=2 * ROWS * 3072 * 240, bytes_accessed=3 * 3072 * 768, transcendentals=0
        ),
    )(lax.axis_index("head").astype(jnp.int32).reshape(1), *parts, gain.reshape(4, 1, columns), wq, wk, wv)


def join_kernel(z, p0, p1, p2, p3, out):
    for place in range(4):
        k = (z[0] + 4 - place) % 4
        part = jnp.where(k < 2, jnp.where(k == 0, p0[...], p1[...]), jnp.where(k == 2, p2[...], p3[...]))
        out[0, :, place * FT : (place + 1) * FT] = part[:, :FT]
        out[1, :, (3 - place) * FT : (4 - place) * FT] = part[:, FT:]


def join(z, parts):
    vmem = pl.BlockSpec(memory_space=pltpu.VMEM)
    return pl.pallas_call(
        join_kernel,
        in_specs=[pl.BlockSpec(memory_space=pltpu.SMEM)] + [vmem] * 4,
        out_specs=vmem,
        out_shape=jax.ShapeDtypeStruct((2, 32, BK), BF16),
        compiler_params=pltpu.CompilerParams(vmem_limit_bytes=2 * 2**20),
        cost_estimate=pl.CostEstimate(flops=0, bytes_accessed=200000, transcendentals=0),
    )(z.astype(jnp.int32).reshape(1), *parts)


def all_latents(half):
    seq = lax.axis_index("seq")

    def place(i):
        return i // 8, (i // 4) % 2, i % 4

    def at(x, y, z):
        return (x * 2 + y) * 4 + z

    def to_y(i):
        x, y, z = place(i)
        return at(x, 1 - y, z)

    def to_z(k, i):
        x, y, z = place(i)
        return at(x, y, (z + k) % 4)

    def to_x(k, i):
        x, y, z = place(i)
        return at((x + k) % 4, y, z)

    parts = [half] + [permute(half, "seq", functools.partial(to_z, k)) for k in (1, 2, 3)]
    block = join(seq % 4, parts)
    pair = jnp.stack([block, permute(block, "seq", to_y)])
    return [pair] + [permute(pair, "seq", functools.partial(to_x, k)) for k in (1, 2, 3)]


def swap(x, bit):
    return permute(x, "head", lambda i: i ^ bit)


def add(a, b):
    return a.astype(F32) + b.astype(F32)


def local(
    latents,
    span_ids,
    patch_weight,
    patch_bias,
    norm_gain,
    query_weight,
    key_weight,
    value_weight,
    out_weight,
):
    seq = lax.axis_index("seq")
    head = lax.axis_index("head")
    half = lax.dynamic_slice_in_dim(latents, (head % 2) * 32, 32, 0)
    halves = all_latents(half)

    b0 = patch_bias.astype(BF16)
    b1 = (patch_bias - b0.astype(F32)).astype(BF16)
    b2 = (patch_bias - b0.astype(F32) - b1.astype(F32)).astype(BF16)
    rest = jnp.zeros((ROWS - 131, patch_bias.shape[0]), BF16)
    wide = jnp.concatenate([patch_weight, b0[None], b1[None], b2[None], rest], axis=0)
    far_part = swap(wide, 2)
    parts = [wide, swap(wide, 1), far_part, swap(far_part, 1)]
    mg, mq, mv = through(parts, norm_gain, query_weight, key_weight, value_weight)
    others = [swap(halves[0], 1)] + [
        swap(lax.optimization_barrier((part, mq))[0], 1) for part in halves[1:]
    ]
    pieces = [piece for pair in zip(halves, others) for piece in pair]

    w_t, _, _ = frequencies()
    spatial = spatial_angles()
    cs = jnp.asarray(np.tile(np.cos(spatial).T, (1, BF)), F32)
    ss = jnp.asarray(np.tile(np.sin(spatial).T, (1, BF)), F32)
    temporal = np.outer(np.arange(FRAMES), w_t)
    by_block = np.repeat(temporal.reshape(NB, BF, 16).transpose(0, 2, 1), FT, axis=2)
    ct = jnp.asarray(np.cos(by_block), F32)
    st = jnp.asarray(np.sin(by_block), F32)
    nothing = np.zeros((FT, 16))
    cq = np.concatenate([nothing, np.cos(spatial)], axis=1)
    sq = np.concatenate([nothing, np.sin(spatial)], axis=1)
    rest = np.zeros((FRAMES, 48))
    tc = np.concatenate([np.cos(temporal), rest], axis=1)
    ts = np.concatenate([np.sin(temporal), rest], axis=1)
    cq = jnp.asarray(np.concatenate([cq, cq], axis=1) * SCALE, F32)
    sq = jnp.asarray(np.concatenate([-sq, sq], axis=1) * SCALE, F32)
    tq = np.stack([np.concatenate([tc, tc], axis=1), np.concatenate([-ts, ts], axis=1)])
    tq = jnp.asarray(tq * SCALE, F32)

    near, near_other, *far, tokens = attention(
        seq.astype(jnp.int32).reshape(1),
        head.astype(jnp.int32).reshape(1),
        span_ids,
        *pieces,
        *(mg, mq, mv, wide, cs, ss, ct, st, cq, sq, tq, out_weight),
    )
    sent = [swap(add(far[i], swap(far[i + 2], 1)).astype(BF16), 2) for i in range(2)]
    kept = add(near, swap(near_other, 1)).astype(BF16)
    return (add(kept, jnp.concatenate(sent)) + tokens.astype(F32)).astype(BF16)


def solution(mesh):
    return jax.shard_map(
        local,
        mesh=mesh,
        in_specs=(
            P(None, "seq"),
            P(),
            P(None, "head"),
            P("head"),
            P(),
            P(None, "head"),
            P(None, "head"),
            P(None, "head"),
            P("head", None),
        ),
        out_specs=P("seq", "head"),
        check_vma=False,
    )
```

```python
import functools
import math

import jax
import jax.numpy as jnp
import numpy as np
from jax import lax
from jax.experimental import pallas as pl
from jax.experimental.pallas import tpu as pltpu
from jax.sharding import PartitionSpec as P

HD = 128
HEADS = 6
FT = 192
FRAMES = 64
BF = 4
BK = BF * FT
NB = FRAMES // BF
ROWS = 144
WIDTH = 24
EPS = 1e-06
YARN = 4.0
SCALE = (0.1 * math.log(YARN) + 1.0) ** 2 / math.sqrt(HD) * math.log2(math.e)
FAR = -1e30
LOW, HIGH = 2.0**-60, 2.0**100

F32 = jnp.float32
BF16 = jnp.bfloat16


def spectrum(count):
    return np.exp(-math.log(10000.0) * np.arange(count) / count)


def frequencies():
    pairs = HD // 2
    count_t, count_h = pairs // 4, 3 * pairs // 8
    base_t = spectrum(count_t)
    ramp = np.clip((FRAMES / 4.0 / (2.0 * math.pi / base_t) - 1.0) / 31.0, 0.0, 1.0)
    return base_t * (ramp + (1.0 - ramp) / YARN), spectrum(count_h), spectrum(pairs - count_t - count_h)


def spatial_angles():
    _, w_h, w_w = frequencies()
    inner = np.arange(FT)
    return np.concatenate(
        [np.outer(inner // WIDTH, w_h), np.outer(inner % WIDTH, w_w)], axis=1
    )


def dot(a, b):
    return jnp.dot(a, b, preferred_element_type=F32)


def kernel(seq_ref, head_ref, span_ref, *refs):
    pieces, refs = refs[:8], refs[8:]
    (mg_ref, mq_ref, mv_ref, pw_ref, cs_ref, ss_ref, ct_ref, st_ref, cq_ref, sq_ref, tq_ref, wo_ref) = refs[:12]
    (outs, tokens_ref), refs = (refs[12:18], refs[18]), refs[19:]
    raw_ref, own_ref, q_ref, w_ref, u_ref, ho_ref, m_ref, k_ref, v_ref, res_ref, wide_ref, sems, out_sems, wide_sem = refs
    seq, head = seq_ref[0], head_ref[0]
    own_frames = (seq, FRAMES - 1 - seq)

    wide_copy = pltpu.make_async_copy(wo_ref, wide_ref, wide_sem)
    wide_copy.start()
    x_at, y_at, core, chip = seq // 8, (seq // 4) % 2, head % 2, head // 2

    copies = []
    for k in range(4):
        for c in range(2):
            rows = pl.ds(pl.multiple_of((core ^ c) * 32, 32), 32)
            for i in range(2):
                group = ((x_at + 4 - k) % 4) * 2 + (y_at ^ i)
                for late in range(2):
                    block = NB - 1 - group if late else group
                    copies.append(
                        pltpu.make_async_copy(
                            pieces[2 * k + c].at[i, late],
                            raw_ref.at[block, rows],
                            sems.at[len(copies)],
                        )
                    )
    for copy in copies:
        copy.start()

    def end_of(frame):
        count = lambda g, seen: seen + (span_ref[g] <= span_ref[frame]).astype(jnp.int32)
        return lax.fori_loop(0, FRAMES, count, 0, unroll=True)

    end_early, end_late = end_of(own_frames[0]), end_of(own_frames[1])
    blocks_early = (end_early + BF - 1) // BF
    blocks_late = (end_late + BF - 1) // BF
    for copy in copies:
        copy.wait()

    row = lax.broadcasted_iota(jnp.int32, (ROWS - 128, BK), 0)
    lane_frame = lax.broadcasted_iota(jnp.int32, (ROWS - 128, BK), 1) // FT
    ones = (row < 3).astype(F32).astype(BF16)

    def features(b):
        now = raw_ref[b]
        last = raw_ref[jnp.maximum(b - 1, 0)][:, BK - FT :]
        last = jnp.where(b > 0, last, jnp.zeros_like(last))
        before = jnp.concatenate([last, now[:, : BK - FT]], axis=1)
        return jnp.concatenate([before, now, ones], axis=0)

    def norm(x, gram):
        y = gram[:ROWS] + gram[ROWS:]
        return lax.rsqrt(jnp.sum(x.astype(F32) * y, axis=0, keepdims=True) + EPS)

    def scaled(x, r):
        tail = jnp.where(row == 0, r, jnp.where(row == 1, 1.0, 0.0))
        return jnp.concatenate([x[:128].astype(F32) * r, tail], axis=0).astype(BF16).T

    def prepare(b):
        inside = jnp.minimum(b, NB - 1)
        x = features(inside)
        big = dot(mg_ref[...], x)
        r = norm(x, big[HEADS * HD :])
        cos = jnp.concatenate([ct_ref[inside], cs_ref[...]], axis=0) * r
        sin = jnp.concatenate([st_ref[inside], ss_ref[...]], axis=0) * r
        cos, sin = cos.astype(BF16), sin.astype(BF16)
        end = jnp.where(row == 0, end_early, end_late)
        mask = jnp.where((row < 2) & (b * BF + lane_frame >= end), FAR, 0.0).astype(BF16)

        def keys(h):
            first, second = big[h * HD : h * HD + 64], big[h * HD + 64 : h * HD + HD]
            first, second = first.astype(BF16), second.astype(BF16)
            return jnp.concatenate(
                [
                    (first * cos - second * sin).astype(BF16),
                    (first * sin + second * cos).astype(BF16),
                    mask,
                ],
                axis=0,
            )

        return keys, lambda: scaled(x, r)

    for i in range(2):
        frame = own_frames[i]
        rows = pl.ds(pl.multiple_of((frame % BF) * FT, FT), FT)
        x = features(frame // BF)
        own_ref[...] = x.T
        res_ref[4, pl.ds(i * FT, FT), :] = dot(own_ref[rows, :], pw_ref[...]).astype(BF16)
        own_ref[...] = scaled(x, norm(x, dot(mg_ref[HEADS * HD :], x)))
        own = own_ref[rows, :]
        lane = lax.broadcasted_iota(jnp.int32, (FT, ROWS - 128), 1)
        select = (lane == i).astype(F32).astype(BF16)
        cos = cq_ref[...] + tq_ref[0, pl.ds(frame, 1), :]
        sin = sq_ref[...] + tq_ref[1, pl.ds(frame, 1), :]
        for h in range(HEADS):
            pre = dot(own, mq_ref[:, pl.ds(h * HD, HD)])
            rotated = pre * cos + pltpu.roll(pre, 64, 1) * sin
            q_ref[i, h] = jnp.concatenate([rotated.astype(BF16), select], axis=1)

    tokens_copy = pltpu.make_async_copy(res_ref.at[4], tokens_ref, out_sems.at[6])
    tokens_copy.start()
    u_ref[...] = jnp.zeros_like(u_ref)

    def fill(b):
        keys, values = prepare(b)
        for h in range(HEADS):
            k_ref[h] = keys(h)
        v_ref[...] = values()

    def visit(frames, b, carry):
        keys, values = prepare(b + 1)
        for h in range(HEADS):
            q = jnp.concatenate([q_ref[i, h] for i in frames], axis=0)
            w = jnp.exp2(dot(q, k_ref[h])).astype(BF16)
            k_ref[h] = keys(h)
            for n, i in enumerate(frames):
                w_ref[i, pl.ds(h * FT, FT)] = w[n * FT : (n + 1) * FT]
        for i in frames:
            u_ref[i] += dot(w_ref[i], v_ref[...])
        v_ref[...] = values()
        return carry

    fill(0)
    lax.fori_loop(0, blocks_early, functools.partial(visit, (0, 1)), 0)
    lax.fori_loop(blocks_early, blocks_late, functools.partial(visit, (1,)), 0)

    def finish():
        good = jnp.ones((FT, 1), F32)
        for i in range(2):
            for h in range(HEADS):
                u = u_ref[i, pl.ds(h * FT, FT)]
                total = u[:, 129:130]
                good = jnp.where((total >= LOW) & (total <= HIGH), good, 0.0)
                mixed = (u / total).astype(BF16)
                ho_ref[pl.ds(i * FT, FT), pl.ds(h * HD, HD)] = dot(
                    mixed, mv_ref[:, pl.ds(h * HD, HD)]
                ).astype(BF16)
        return jnp.min(good) > 0.5

    bad = jnp.logical_not(finish())

    @pl.when(bad)
    def _():
        u_ref[...] = jnp.zeros_like(u_ref)
        m_ref[...] = jnp.full_like(m_ref, FAR)

        def visit_again(b, carry):
            fill(b)
            for h in range(HEADS):
                k = k_ref[h]
                rows = pl.ds(h * FT, FT)
                for i in range(2):
                    s = dot(q_ref[i, h], k)
                    old = m_ref[i, rows]
                    new = jnp.maximum(old, jnp.max(s, axis=1, keepdims=True))
                    w = jnp.exp2(s - new).astype(BF16)
                    u_ref[i, rows] = u_ref[i, rows] * jnp.exp2(old - new) + dot(w, v_ref[...])
                    m_ref[i, rows] = new
            return carry

        lax.fori_loop(0, blocks_late, visit_again, 0)
        finish()

    sent = [tokens_copy]
    wide_copy.wait()
    for n in (3, 2, 1, 0):
        group = (chip ^ (n // 2)) * 2 + (core ^ (n % 2))
        columns = pl.ds(pl.multiple_of(group * 768, 768), 768)
        res_ref[n] = dot(ho_ref[...], wide_ref[:, columns]).astype(BF16)
        for i, target in enumerate(outs[2 * n - 2 : 2 * n] if n > 1 else outs[n : n + 1]):
            source = res_ref.at[n, pl.ds(i * FT, FT)] if n > 1 else res_ref.at[n]
            sent.append(pltpu.make_async_copy(source, target, out_sems.at[len(sent) - 1]))
            sent[-1].start()
    for copy in sent:
        copy.wait()


def attention(*arrays):
    vmem = pl.BlockSpec(memory_space=pltpu.VMEM)
    hbm = pl.BlockSpec(memory_space=pl.ANY)
    shape = jax.ShapeDtypeStruct((2 * FT, 768), BF16)
    frame = jax.ShapeDtypeStruct((FT, 768), BF16)
    return pl.pallas_call(
        kernel,
        in_specs=[pl.BlockSpec(memory_space=pltpu.SMEM)] * 3 + [hbm] * 8 + [vmem] * 11 + [hbm],
        out_specs=(hbm,) * 7,
        out_shape=(shape,) * 2 + (frame,) * 4 + (shape,),
        scratch_shapes=[
            pltpu.VMEM((NB, 64, BK), BF16),
            pltpu.VMEM((BK, ROWS), BF16),
            pltpu.VMEM((2, HEADS, FT, ROWS), BF16),
            pltpu.VMEM((2, HEADS * FT, BK), BF16),
            pltpu.VMEM((2, HEADS * FT, ROWS), F32),
            pltpu.VMEM((2 * FT, HEADS * HD), BF16),
            pltpu.VMEM((2, HEADS * FT, 1), F32),
            pltpu.VMEM((HEADS, ROWS, BK), BF16),
            pltpu.VMEM((BK, ROWS), BF16),
            pltpu.VMEM((5, 2 * FT, HEADS * HD), BF16),
            pltpu.VMEM((HEADS * HD, 4 * HEADS * HD), BF16),
            pltpu.SemaphoreType.DMA((32,)),
            pltpu.SemaphoreType.DMA((7,)),
            pltpu.SemaphoreType.DMA,
        ],
        compiler_params=pltpu.CompilerParams(vmem_limit_bytes=52 * 2**20),
    )(*arrays)


def permute(x, axis, to):
    return lax.ppermute(x, axis, [(i, to(i)) for i in range(lax.axis_size(axis))])


def weights_kernel(me, p0, p1, p2, p3, gain, wq, wk, wv, mg_ref, mq_ref, mv_ref, aq, ak, av, ag):
    k = pl.program_id(0)

    @pl.when(k == 0)
    def _():
        for ref in (aq, ak, av, ag):
            ref[...] = jnp.zeros_like(ref)

    part = jnp.where(k < 2, jnp.where(k == 0, p0[...], p1[...]), jnp.where(k == 2, p2[...], p3[...]))
    wide = part.astype(F32)
    bias = wide[128:129] + wide[129:130] + wide[130:131]
    row = lax.broadcasted_iota(jnp.int32, (ROWS - 128, part.shape[1]), 0)
    gained = jnp.concatenate([wide[:128], jnp.where(row == 0, bias, 0.0)], axis=0) * gain[0]
    gained = gained.astype(BF16)
    aq[...] += dot(gained, wq[...])
    ak[...] += dot(gained, wk[...])
    av[...] += dot(gained, wv[...])
    ag[...] += lax.dot_general(part, part, (((1,), (1,)), ((), ())), preferred_element_type=F32)

    @pl.when(k == 3)
    def _():
        mq_ref[...] = aq[...].astype(BF16)
        mv_ref[...] = av[...].astype(BF16)
        mg_ref[: HEADS * HD, :] = ak[...].T.astype(BF16)
        gram = ag[...] * (1.0 / (4 * part.shape[1]))
        high = gram.astype(BF16)
        mg_ref[HEADS * HD : HEADS * HD + ROWS, :] = high
        mg_ref[HEADS * HD + ROWS :, :] = (gram - high.astype(F32)).astype(BF16)


def through(parts, gain, wq, wk, wv):
    columns = HEADS * HD
    whole = lambda *shape: pl.BlockSpec(shape, lambda k, me: (0,) * len(shape))
    source = lambda k, me: me[0] ^ k
    weight = pl.BlockSpec((columns, columns), lambda k, me: (source(k, me), 0))
    return pl.pallas_call(
        weights_kernel,
        grid_spec=pltpu.PrefetchScalarGridSpec(
            num_scalar_prefetch=1,
            grid=(4,),
            in_specs=[whole(ROWS, columns)] * 4
            + [pl.BlockSpec((1, 1, columns), lambda k, me: (source(k, me), 0, 0))]
            + [weight] * 3,
            out_specs=[
                whole(columns + 2 * ROWS, ROWS),
                whole(ROWS, columns),
                whole(ROWS, columns),
            ],
            scratch_shapes=[pltpu.VMEM((ROWS, columns), F32)] * 3 + [pltpu.VMEM((ROWS, ROWS), F32)],
        ),
        out_shape=[
            jax.ShapeDtypeStruct((columns + 2 * ROWS, ROWS), BF16),
            jax.ShapeDtypeStruct((ROWS, columns), BF16),
            jax.ShapeDtypeStruct((ROWS, columns), BF16),
        ],
        compiler_params=pltpu.CompilerParams(vmem_limit_bytes=57 * 2**20),
        cost_estimate=pl.CostEstimate(
            flops=2 * ROWS * 3072 * 240, bytes_accessed=3 * 3072 * 768, transcendentals=0
        ),
    )(lax.axis_index("head").astype(jnp.int32).reshape(1), *parts, gain.reshape(4, 1, columns), wq, wk, wv)


def join_kernel(z, p0, p1, p2, p3, out):
    for place in range(4):
        k = (z[0] + 4 - place) % 4
        part = jnp.where(k < 2, jnp.where(k == 0, p0[...], p1[...]), jnp.where(k == 2, p2[...], p3[...]))
        out[0, :, place * FT : (place + 1) * FT] = part[:, :FT]
        out[1, :, (3 - place) * FT : (4 - place) * FT] = part[:, FT:]


def join(z, parts):
    vmem = pl.BlockSpec(memory_space=pltpu.VMEM)
    return pl.pallas_call(
        join_kernel,
        in_specs=[pl.BlockSpec(memory_space=pltpu.SMEM)] + [vmem] * 4,
        out_specs=vmem,
        out_shape=jax.ShapeDtypeStruct((2, 32, BK), BF16),
        compiler_params=pltpu.CompilerParams(vmem_limit_bytes=2 * 2**20),
        cost_estimate=pl.CostEstimate(flops=0, bytes_accessed=200000, transcendentals=0),
    )(z.astype(jnp.int32).reshape(1), *parts)


def all_latents(half):
    seq = lax.axis_index("seq")

    def place(i):
        return i // 8, (i // 4) % 2, i % 4

    def at(x, y, z):
        return (x * 2 + y) * 4 + z

    def to_y(i):
        x, y, z = place(i)
        return at(x, 1 - y, z)

    def to_z(k, i):
        x, y, z = place(i)
        return at(x, y, (z + k) % 4)

    def to_x(k, i):
        x, y, z = place(i)
        return at((x + k) % 4, y, z)

    parts = [half] + [permute(half, "seq", functools.partial(to_z, k)) for k in (1, 2, 3)]
    block = join(seq % 4, parts)
    pair = jnp.stack([block, permute(block, "seq", to_y)])
    return block, [pair] + [permute(pair, "seq", functools.partial(to_x, k)) for k in (1, 2, 3)]


def swap(x, bit):
    return permute(x, "head", lambda i: i ^ bit)


def add(a, b):
    return a.astype(F32) + b.astype(F32)


def local(
    latents,
    span_ids,
    patch_weight,
    patch_bias,
    norm_gain,
    query_weight,
    key_weight,
    value_weight,
    out_weight,
):
    seq = lax.axis_index("seq")
    head = lax.axis_index("head")
    half = lax.dynamic_slice_in_dim(latents, (head % 2) * 32, 32, 0)
    joined, halves = all_latents(half)

    b0 = patch_bias.astype(BF16)
    b1 = (patch_bias - b0.astype(F32)).astype(BF16)
    b2 = (patch_bias - b0.astype(F32) - b1.astype(F32)).astype(BF16)
    rest = jnp.zeros((ROWS - 131, patch_bias.shape[0]), BF16)
    wide = jnp.concatenate([patch_weight, b0[None], b1[None], b2[None], rest], axis=0)
    ready = lax.optimization_barrier((wide, joined))[0]
    far_part = swap(ready, 2)
    parts = [wide, swap(ready, 1), far_part, swap(far_part, 1)]
    mg, mq, mv = through(parts, norm_gain, query_weight, key_weight, value_weight)
    others = [swap(halves[0], 1)] + [
        swap(lax.optimization_barrier((part, mq))[0], 1) for part in halves[1:]
    ]
    pieces = [piece for pair in zip(halves, others) for piece in pair]

    w_t, _, _ = frequencies()
    spatial = spatial_angles()
    cs = jnp.asarray(np.tile(np.cos(spatial).T, (1, BF)), F32)
    ss = jnp.asarray(np.tile(np.sin(spatial).T, (1, BF)), F32)
    temporal = np.outer(np.arange(FRAMES), w_t)
    by_block = np.repeat(temporal.reshape(NB, BF, 16).transpose(0, 2, 1), FT, axis=2)
    ct = jnp.asarray(np.cos(by_block), F32)
    st = jnp.asarray(np.sin(by_block), F32)
    nothing = np.zeros((FT, 16))
    cq = np.concatenate([nothing, np.cos(spatial)], axis=1)
    sq = np.concatenate([nothing, np.sin(spatial)], axis=1)
    rest = np.zeros((FRAMES, 48))
    tc = np.concatenate([np.cos(temporal), rest], axis=1)
    ts = np.concatenate([np.sin(temporal), rest], axis=1)
    cq = jnp.asarray(np.concatenate([cq, cq], axis=1) * SCALE, F32)
    sq = jnp.asarray(np.concatenate([-sq, sq], axis=1) * SCALE, F32)
    tq = np.stack([np.concatenate([tc, tc], axis=1), np.concatenate([-ts, ts], axis=1)])
    tq = jnp.asarray(tq * SCALE, F32)

    near, near_other, *far, tokens = attention(
        seq.astype(jnp.int32).reshape(1),
        head.astype(jnp.int32).reshape(1),
        span_ids,
        *pieces,
        *(mg, mq, mv, wide, cs, ss, ct, st, cq, sq, tq, out_weight),
    )
    sent = [swap(add(far[i], swap(far[i + 2], 1)).astype(BF16), 2) for i in range(2)]
    kept = add(near, swap(near_other, 1)).astype(BF16)
    return (add(kept, jnp.concatenate(sent)) + tokens.astype(F32)).astype(BF16)


def solution(mesh):
    return jax.shard_map(
        local,
        mesh=mesh,
        in_specs=(
            P(None, "seq"),
            P(),
            P(None, "head"),
            P("head"),
            P(),
            P(None, "head"),
            P(None, "head"),
            P(None, "head"),
            P("head", None),
        ),
        out_specs=P("seq", "head"),
        check_vma=False,
    )
```

```python
import functools
import math

import jax
import jax.numpy as jnp
import numpy as np
from jax import lax
from jax.experimental import pallas as pl
from jax.experimental.pallas import tpu as pltpu
from jax.sharding import PartitionSpec as P

HD = 128
HEADS = 6
FT = 192
FRAMES = 64
BF = 4
BK = BF * FT
NB = FRAMES // BF
ROWS = 144
WIDTH = 24
EPS = 1e-06
YARN = 4.0
SCALE = (0.1 * math.log(YARN) + 1.0) ** 2 / math.sqrt(HD) * math.log2(math.e)
FAR = -1e30
LOW, HIGH = 2.0**-60, 2.0**100

F32 = jnp.float32
BF16 = jnp.bfloat16


def spectrum(count):
    return np.exp(-math.log(10000.0) * np.arange(count) / count)


def frequencies():
    pairs = HD // 2
    count_t, count_h = pairs // 4, 3 * pairs // 8
    base_t = spectrum(count_t)
    ramp = np.clip((FRAMES / 4.0 / (2.0 * math.pi / base_t) - 1.0) / 31.0, 0.0, 1.0)
    return base_t * (ramp + (1.0 - ramp) / YARN), spectrum(count_h), spectrum(pairs - count_t - count_h)


def spatial_angles():
    _, w_h, w_w = frequencies()
    inner = np.arange(FT)
    return np.concatenate(
        [np.outer(inner // WIDTH, w_h), np.outer(inner % WIDTH, w_w)], axis=1
    )


def dot(a, b):
    return jnp.dot(a, b, preferred_element_type=F32)


def kernel(seq_ref, head_ref, span_ref, *refs):
    pieces, refs = refs[:8], refs[8:]
    (mg_ref, mq_ref, mv_ref, pw_ref, cs_ref, ss_ref, ct_ref, st_ref, cq_ref, sq_ref, tq_ref, wo_ref) = refs[:12]
    (outs, tokens_ref), refs = (refs[12:18], refs[18]), refs[19:]
    raw_ref, own_ref, q_ref, w_ref, u_ref, ho_ref, m_ref, k_ref, v_ref, res_ref, wide_ref, sems, out_sems, wide_sem = refs
    seq, head = seq_ref[0], head_ref[0]
    own_frames = (seq, FRAMES - 1 - seq)

    wide_copy = pltpu.make_async_copy(wo_ref, wide_ref, wide_sem)
    wide_copy.start()
    x_at, y_at, core, chip = seq // 8, (seq // 4) % 2, head % 2, head // 2

    copies = []
    for k in range(4):
        for c in range(2):
            rows = pl.ds(pl.multiple_of((core ^ c) * 32, 32), 32)
            for i in range(2):
                group = ((x_at + 4 - k) % 4) * 2 + (y_at ^ i)
                for late in range(2):
                    block = NB - 1 - group if late else group
                    copies.append(
                        pltpu.make_async_copy(
                            pieces[2 * k + c].at[i, late],
                            raw_ref.at[block, rows],
                            sems.at[len(copies)],
                        )
                    )
    for copy in copies:
        copy.start()

    def end_of(frame):
        count = lambda g, seen: seen + (span_ref[g] <= span_ref[frame]).astype(jnp.int32)
        return lax.fori_loop(0, FRAMES, count, 0, unroll=True)

    end_early, end_late = end_of(own_frames[0]), end_of(own_frames[1])
    blocks_early = (end_early + BF - 1) // BF
    blocks_late = (end_late + BF - 1) // BF
    for copy in copies:
        copy.wait()

    row = lax.broadcasted_iota(jnp.int32, (ROWS - 128, BK), 0)
    lane_frame = lax.broadcasted_iota(jnp.int32, (ROWS - 128, BK), 1) // FT
    ones = (row < 3).astype(F32).astype(BF16)

    def features(b):
        now = raw_ref[b]
        last = raw_ref[jnp.maximum(b - 1, 0)][:, BK - FT :]
        last = jnp.where(b > 0, last, jnp.zeros_like(last))
        before = jnp.concatenate([last, now[:, : BK - FT]], axis=1)
        return jnp.concatenate([before, now, ones], axis=0)

    def norm(x, gram):
        y = gram[:ROWS] + gram[ROWS:]
        return lax.rsqrt(jnp.sum(x.astype(F32) * y, axis=0, keepdims=True) + EPS)

    def scaled(x, r):
        tail = jnp.where(row == 0, r, jnp.where(row == 1, 1.0, 0.0))
        return jnp.concatenate([x[:128].astype(F32) * r, tail], axis=0).astype(BF16).T

    def prepare(b):
        inside = jnp.minimum(b, NB - 1)
        x = features(inside)
        big = dot(mg_ref[...], x)
        r = norm(x, big[HEADS * HD :])
        cos = jnp.concatenate([ct_ref[inside], cs_ref[...]], axis=0) * r
        sin = jnp.concatenate([st_ref[inside], ss_ref[...]], axis=0) * r
        cos, sin = cos.astype(BF16), sin.astype(BF16)
        end = jnp.where(row == 0, end_early, end_late)
        mask = jnp.where((row < 2) & (b * BF + lane_frame >= end), FAR, 0.0).astype(BF16)

        def keys(h):
            first, second = big[h * HD : h * HD + 64], big[h * HD + 64 : h * HD + HD]
            first, second = first.astype(BF16), second.astype(BF16)
            return jnp.concatenate(
                [
                    (first * cos - second * sin).astype(BF16),
                    (first * sin + second * cos).astype(BF16),
                    mask,
                ],
                axis=0,
            )

        return keys, lambda: scaled(x, r)

    for i in range(2):
        frame = own_frames[i]
        rows = pl.ds(pl.multiple_of((frame % BF) * FT, FT), FT)
        x = features(frame // BF)
        own_ref[...] = x.T
        res_ref[4, pl.ds(i * FT, FT), :] = dot(own_ref[rows, :], pw_ref[...]).astype(BF16)
        own_ref[...] = scaled(x, norm(x, dot(mg_ref[HEADS * HD :], x)))
        own = own_ref[rows, :]
        lane = lax.broadcasted_iota(jnp.int32, (FT, ROWS - 128), 1)
        select = (lane == i).astype(F32).astype(BF16)
        cos = cq_ref[...] + tq_ref[0, pl.ds(frame, 1), :]
        sin = sq_ref[...] + tq_ref[1, pl.ds(frame, 1), :]
        for h in range(HEADS):
            pre = dot(own, mq_ref[:, pl.ds(h * HD, HD)])
            rotated = pre * cos + pltpu.roll(pre, 64, 1) * sin
            q_ref[i, h] = jnp.concatenate([rotated.astype(BF16), select], axis=1)

    tokens_copy = pltpu.make_async_copy(res_ref.at[4], tokens_ref, out_sems.at[6])
    tokens_copy.start()
    u_ref[...] = jnp.zeros_like(u_ref)

    def fill(b):
        keys, values = prepare(b)
        for h in range(HEADS):
            k_ref[h] = keys(h)
        v_ref[...] = values()

    def visit(frames, b, carry):
        keys, values = prepare(b + 1)
        for h in range(HEADS):
            q = jnp.concatenate([q_ref[i, h] for i in frames], axis=0)
            w = jnp.exp2(dot(q, k_ref[h])).astype(BF16)
            k_ref[h] = keys(h)
            for n, i in enumerate(frames):
                w_ref[i, pl.ds(h * FT, FT)] = w[n * FT : (n + 1) * FT]
        for i in frames:
            u_ref[i] += dot(w_ref[i], v_ref[...])
        v_ref[...] = values()
        return carry

    fill(0)
    lax.fori_loop(0, blocks_early, functools.partial(visit, (0, 1)), 0)
    lax.fori_loop(blocks_early, blocks_late, functools.partial(visit, (1,)), 0)

    def finish():
        good = jnp.ones((FT, 1), F32)
        for i in range(2):
            for h in range(HEADS):
                u = u_ref[i, pl.ds(h * FT, FT)]
                total = u[:, 129:130]
                good = jnp.where((total >= LOW) & (total <= HIGH), good, 0.0)
                mixed = (u / total).astype(BF16)
                ho_ref[pl.ds(i * FT, FT), pl.ds(h * HD, HD)] = dot(
                    mixed, mv_ref[:, pl.ds(h * HD, HD)]
                ).astype(BF16)
        return jnp.min(good) > 0.5

    bad = jnp.logical_not(finish())

    @pl.when(bad)
    def _():
        u_ref[...] = jnp.zeros_like(u_ref)
        m_ref[...] = jnp.full_like(m_ref, FAR)

        def visit_again(b, carry):
            fill(b)
            for h in range(HEADS):
                k = k_ref[h]
                rows = pl.ds(h * FT, FT)
                for i in range(2):
                    s = dot(q_ref[i, h], k)
                    old = m_ref[i, rows]
                    new = jnp.maximum(old, jnp.max(s, axis=1, keepdims=True))
                    w = jnp.exp2(s - new).astype(BF16)
                    u_ref[i, rows] = u_ref[i, rows] * jnp.exp2(old - new) + dot(w, v_ref[...])
                    m_ref[i, rows] = new
            return carry

        lax.fori_loop(0, blocks_late, visit_again, 0)
        finish()

    sent = [tokens_copy]
    wide_copy.wait()
    for n in (3, 2, 1, 0):
        group = (chip ^ (n // 2)) * 2 + (core ^ (n % 2))
        columns = pl.ds(pl.multiple_of(group * 768, 768), 768)
        res_ref[n] = dot(ho_ref[...], wide_ref[:, columns]).astype(BF16)
        for i, target in enumerate(outs[2 * n - 2 : 2 * n] if n > 1 else outs[n : n + 1]):
            source = res_ref.at[n, pl.ds(i * FT, FT)] if n > 1 else res_ref.at[n]
            sent.append(pltpu.make_async_copy(source, target, out_sems.at[len(sent) - 1]))
            sent[-1].start()
    for copy in sent:
        copy.wait()


def attention(*arrays):
    vmem = pl.BlockSpec(memory_space=pltpu.VMEM)
    hbm = pl.BlockSpec(memory_space=pl.ANY)
    shape = jax.ShapeDtypeStruct((2 * FT, 768), BF16)
    frame = jax.ShapeDtypeStruct((FT, 768), BF16)
    return pl.pallas_call(
        kernel,
        in_specs=[pl.BlockSpec(memory_space=pltpu.SMEM)] * 3 + [hbm] * 8 + [vmem] * 11 + [hbm],
        out_specs=(hbm,) * 7,
        out_shape=(shape,) * 2 + (frame,) * 4 + (shape,),
        scratch_shapes=[
            pltpu.VMEM((NB, 64, BK), BF16),
            pltpu.VMEM((BK, ROWS), BF16),
            pltpu.VMEM((2, HEADS, FT, ROWS), BF16),
            pltpu.VMEM((2, HEADS * FT, BK), BF16),
            pltpu.VMEM((2, HEADS * FT, ROWS), F32),
            pltpu.VMEM((2 * FT, HEADS * HD), BF16),
            pltpu.VMEM((2, HEADS * FT, 1), F32),
            pltpu.VMEM((HEADS, ROWS, BK), BF16),
            pltpu.VMEM((BK, ROWS), BF16),
            pltpu.VMEM((5, 2 * FT, HEADS * HD), BF16),
            pltpu.VMEM((HEADS * HD, 4 * HEADS * HD), BF16),
            pltpu.SemaphoreType.DMA((32,)),
            pltpu.SemaphoreType.DMA((7,)),
            pltpu.SemaphoreType.DMA,
        ],
        compiler_params=pltpu.CompilerParams(vmem_limit_bytes=52 * 2**20),
    )(*arrays)


def permute(x, axis, to):
    return lax.ppermute(x, axis, [(i, to(i)) for i in range(lax.axis_size(axis))])


def weights_kernel(me, p0, p1, p2, p3, gain, wq, wk, wv, mg_ref, mq_ref, mv_ref, aq, ak, av, ag):
    k = pl.program_id(0)

    @pl.when(k == 0)
    def _():
        for ref in (aq, ak, av, ag):
            ref[...] = jnp.zeros_like(ref)

    n, half = k // 2, pl.ds(pl.multiple_of((k % 2) * wq.shape[0], 128), wq.shape[0])
    part = jnp.where(
        n < 2, jnp.where(n == 0, p0[:, half], p1[:, half]), jnp.where(n == 2, p2[:, half], p3[:, half])
    )
    wide = part.astype(F32)
    bias = wide[128:129] + wide[129:130] + wide[130:131]
    row = lax.broadcasted_iota(jnp.int32, (ROWS - 128, part.shape[1]), 0)
    gained = jnp.concatenate([wide[:128], jnp.where(row == 0, bias, 0.0)], axis=0) * gain[0]
    gained = gained.astype(BF16)
    aq[...] += dot(gained, wq[...])
    ak[...] += dot(gained, wk[...])
    av[...] += dot(gained, wv[...])
    ag[...] += lax.dot_general(part, part, (((1,), (1,)), ((), ())), preferred_element_type=F32)

    @pl.when(k == 7)
    def _():
        mq_ref[...] = aq[...].astype(BF16)
        mv_ref[...] = av[...].astype(BF16)
        mg_ref[: HEADS * HD, :] = ak[...].T.astype(BF16)
        gram = ag[...] * (1.0 / (8 * part.shape[1]))
        high = gram.astype(BF16)
        mg_ref[HEADS * HD : HEADS * HD + ROWS, :] = high
        mg_ref[HEADS * HD + ROWS :, :] = (gram - high.astype(F32)).astype(BF16)


def through(parts, gain, wq, wk, wv):
    columns = HEADS * HD
    whole = lambda *shape: pl.BlockSpec(shape, lambda k, me: (0,) * len(shape))
    source = lambda k, me: (me[0] ^ (k // 2)) * 2 + k % 2
    weight = pl.BlockSpec((columns // 2, columns), lambda k, me: (source(k, me), 0))
    return pl.pallas_call(
        weights_kernel,
        grid_spec=pltpu.PrefetchScalarGridSpec(
            num_scalar_prefetch=1,
            grid=(8,),
            in_specs=[whole(ROWS, columns)] * 4
            + [pl.BlockSpec((1, 1, columns // 2), lambda k, me: (source(k, me), 0, 0))]
            + [weight] * 3,
            out_specs=[
                whole(columns + 2 * ROWS, ROWS),
                whole(ROWS, columns),
                whole(ROWS, columns),
            ],
            scratch_shapes=[pltpu.VMEM((ROWS, columns), F32)] * 3 + [pltpu.VMEM((ROWS, ROWS), F32)],
        ),
        out_shape=[
            jax.ShapeDtypeStruct((columns + 2 * ROWS, ROWS), BF16),
            jax.ShapeDtypeStruct((ROWS, columns), BF16),
            jax.ShapeDtypeStruct((ROWS, columns), BF16),
        ],
        compiler_params=pltpu.CompilerParams(vmem_limit_bytes=57 * 2**20),
        cost_estimate=pl.CostEstimate(
            flops=2 * ROWS * 3072 * 240, bytes_accessed=3 * 3072 * 768, transcendentals=0
        ),
    )(lax.axis_index("head").astype(jnp.int32).reshape(1), *parts, gain.reshape(8, 1, columns // 2), wq, wk, wv)


def join_kernel(z, p0, p1, p2, p3, out):
    for place in range(4):
        k = (z[0] + 4 - place) % 4
        part = jnp.where(k < 2, jnp.where(k == 0, p0[...], p1[...]), jnp.where(k == 2, p2[...], p3[...]))
        out[0, :, place * FT : (place + 1) * FT] = part[:, :FT]
        out[1, :, (3 - place) * FT : (4 - place) * FT] = part[:, FT:]


def join(z, parts):
    vmem = pl.BlockSpec(memory_space=pltpu.VMEM)
    return pl.pallas_call(
        join_kernel,
        in_specs=[pl.BlockSpec(memory_space=pltpu.SMEM)] + [vmem] * 4,
        out_specs=vmem,
        out_shape=jax.ShapeDtypeStruct((2, 32, BK), BF16),
        compiler_params=pltpu.CompilerParams(vmem_limit_bytes=2 * 2**20),
        cost_estimate=pl.CostEstimate(flops=0, bytes_accessed=200000, transcendentals=0),
    )(z.astype(jnp.int32).reshape(1), *parts)


def all_latents(half):
    seq = lax.axis_index("seq")

    def place(i):
        return i // 8, (i // 4) % 2, i % 4

    def at(x, y, z):
        return (x * 2 + y) * 4 + z

    def to_y(i):
        x, y, z = place(i)
        return at(x, 1 - y, z)

    def to_z(k, i):
        x, y, z = place(i)
        return at(x, y, (z + k) % 4)

    def to_x(k, i):
        x, y, z = place(i)
        return at((x + k) % 4, y, z)

    parts = [half] + [permute(half, "seq", functools.partial(to_z, k)) for k in (1, 2, 3)]
    block = join(seq % 4, parts)
    pair = jnp.stack([block, permute(block, "seq", to_y)])
    return [pair] + [permute(pair, "seq", functools.partial(to_x, k)) for k in (1, 2, 3)]


def swap(x, bit):
    return permute(x, "head", lambda i: i ^ bit)


def add(a, b):
    return a.astype(F32) + b.astype(F32)


def local(
    latents,
    span_ids,
    patch_weight,
    patch_bias,
    norm_gain,
    query_weight,
    key_weight,
    value_weight,
    out_weight,
):
    seq = lax.axis_index("seq")
    head = lax.axis_index("head")
    half = lax.dynamic_slice_in_dim(latents, (head % 2) * 32, 32, 0)
    halves = all_latents(half)

    b0 = patch_bias.astype(BF16)
    b1 = (patch_bias - b0.astype(F32)).astype(BF16)
    b2 = (patch_bias - b0.astype(F32) - b1.astype(F32)).astype(BF16)
    rest = jnp.zeros((ROWS - 131, patch_bias.shape[0]), BF16)
    wide = jnp.concatenate([patch_weight, b0[None], b1[None], b2[None], rest], axis=0)
    far_part = swap(wide, 2)
    parts = [wide, swap(wide, 1), far_part, swap(far_part, 1)]
    mg, mq, mv = through(parts, norm_gain, query_weight, key_weight, value_weight)
    others = [swap(halves[0], 1)] + [
        swap(lax.optimization_barrier((part, mq))[0], 1) for part in halves[1:]
    ]
    pieces = [piece for pair in zip(halves, others) for piece in pair]

    w_t, _, _ = frequencies()
    spatial = spatial_angles()
    cs = jnp.asarray(np.tile(np.cos(spatial).T, (1, BF)), F32)
    ss = jnp.asarray(np.tile(np.sin(spatial).T, (1, BF)), F32)
    temporal = np.outer(np.arange(FRAMES), w_t)
    by_block = np.repeat(temporal.reshape(NB, BF, 16).transpose(0, 2, 1), FT, axis=2)
    ct = jnp.asarray(np.cos(by_block), F32)
    st = jnp.asarray(np.sin(by_block), F32)
    nothing = np.zeros((FT, 16))
    cq = np.concatenate([nothing, np.cos(spatial)], axis=1)
    sq = np.concatenate([nothing, np.sin(spatial)], axis=1)
    rest = np.zeros((FRAMES, 48))
    tc = np.concatenate([np.cos(temporal), rest], axis=1)
    ts = np.concatenate([np.sin(temporal), rest], axis=1)
    cq = jnp.asarray(np.concatenate([cq, cq], axis=1) * SCALE, F32)
    sq = jnp.asarray(np.concatenate([-sq, sq], axis=1) * SCALE, F32)
    tq = np.stack([np.concatenate([tc, tc], axis=1), np.concatenate([-ts, ts], axis=1)])
    tq = jnp.asarray(tq * SCALE, F32)

    near, near_other, *far, tokens = attention(
        seq.astype(jnp.int32).reshape(1),
        head.astype(jnp.int32).reshape(1),
        span_ids,
        *pieces,
        *(mg, mq, mv, wide, cs, ss, ct, st, cq, sq, tq, out_weight),
    )
    sent = [swap(add(far[i], swap(far[i + 2], 1)).astype(BF16), 2) for i in range(2)]
    kept = add(near, swap(near_other, 1)).astype(BF16)
    return (add(kept, jnp.concatenate(sent)) + tokens.astype(F32)).astype(BF16)


def solution(mesh):
    return jax.shard_map(
        local,
        mesh=mesh,
        in_specs=(
            P(None, "seq"),
            P(),
            P(None, "head"),
            P("head"),
            P(),
            P(None, "head"),
            P(None, "head"),
            P(None, "head"),
            P("head", None),
        ),
        out_specs=P("seq", "head"),
        check_vma=False,
    )
```
